256 devices in a mesh: seq: 16 (over x_hi, y, core), grp: 16 (over x_lo, z).
Axes of the slice: x: 4 (x_hi: 2, x_lo: 2; x = x_hi * 2 + x_lo), y: 4, z: 8, core: 2. Of those that a mesh axis runs over, the one named last changes fastest.
Arguments:
- gate_in: bfloat16 [8192, 8192], P('seq', 'grp'), may hold values from 0.5 to 1.5
- key_in: bfloat16 [8192, 8192], P('seq', 'grp'), may hold values from -12 to 12, as said below
- value_in: bfloat16 [8192, 8192], P('seq', 'grp'), may hold values from 0.5 to 1.5
- filt_in: bfloat16 [8192, 8192], P('seq', 'grp'), may hold values from -1 to 1
- skip_gain: float32 [8192], P('grp'), may hold values from -3 to 3
- running_gram: float32 [8192, 8192], P('seq', 'grp'), may hold values from -2 to 2
Outputs:
- gram: float32 [8192, 8192], P('seq', 'grp')
The draws below stay inside these ranges and needn't reach their ends.
Inputs may be any that keep to these rules, and one draw needn't show every extreme that they name: `key_in`: each row (token) is a value shared by all channels of that token plus independent per-channel parts.
All inputs are finite; a program needn't handle non-finite values.
Results may differ from the reference program's by a relative error of at most 0.0012.
Values may be sent and summed in bfloat16 or wider, within the bound.
No kernel may reach another device: no remote copies, remote signals or barrier semaphores. Data moves between devices by JAX's collectives and lax.ppermute only.
A program may use at most 128 MiB of HBM per device.

```python
import math
import jax
import jax.numpy as jnp
from jax import lax

D = 8192
LENGTH = 8192
N_SEQ = 16


def energy_scale(rates, count):
    return jnp.sqrt(jnp.expm1(-2.0 * rates) / jnp.expm1(-2.0 * rates * count))


def draw_filt_in(key, part):
    key = jax.random.fold_in(key, 7)
    first, second, third = jax.random.split(key, 3)
    spread = jax.random.uniform(first, (1, D), jnp.float32)
    lowest = jnp.log(0.5 / LENGTH)
    highest = jnp.log(1.0 / 30)
    rates = jnp.exp(lowest + spread * (highest - lowest))
    slow_rate = jnp.full((1, D), 0.5 / LENGTH, jnp.float32)
    steps_t = jnp.arange(LENGTH, dtype=jnp.float32)[:, None]
    head = energy_scale(rates, LENGTH) * jnp.exp(-rates * steps_t)
    tail = energy_scale(slow_rate, LENGTH) * jnp.exp(-slow_rate * steps_t)
    mix_draw = jax.random.uniform(third, (1, D), jnp.float32)
    share = jnp.exp(jnp.log(0.05) + mix_draw * (jnp.log(0.3) - jnp.log(0.05)))
    noise = jnp.clip(jax.random.normal(second, (LENGTH, D), jnp.float32), -3.9, 3.9)
    envelope = jnp.sqrt(1.0 - share) * head + jnp.sqrt(share) * tail
    values = noise * envelope
    return jnp.clip(values, -1.0, 1.0).astype(jnp.bfloat16)


def draw_key_in(key, part):
    key = jax.random.fold_in(key, 3)
    first, second = jax.random.split(key)
    shared = jnp.clip(jax.random.normal(first, (LENGTH, 1), jnp.float32), -5.0, 5.0)
    noise = jnp.clip(jax.random.normal(second, (LENGTH, D), jnp.float32), -6.0, 6.0)
    return jnp.clip(shared + 0.7 * noise, -12.0, 12.0).astype(jnp.bfloat16)


def block_scale(rng, extent, pieces, least, top_value):
    def one(position, shards_of):
        draws = jax.random.uniform(jax.random.fold_in(jax.random.fold_in(rng, 6), position), (shards_of,), jnp.float32, least / len(pieces), top_value / len(pieces))
        return jnp.repeat(jnp.exp(draws), extent[position] // shards_of).reshape((-1,) + (1,) * (len(extent) - position - 1))

    gain = one(*pieces[0])
    for cut in pieces[1:]:
        gain = gain * one(*cut)
    return gain


def centred(rng, dims, deviation, reach, cuts=(), kind=jnp.bfloat16):
    values = deviation * jax.random.normal(rng, dims, jnp.float32)
    if cuts:
        values = values * block_scale(rng, dims, cuts, -0.22, 0.18)
    return jnp.clip(values, -reach, reach).astype(kind)


def setup_inputs(seed: int = 0) -> dict:
    arg_keys = jax.random.split(jax.random.key(seed), 7)
    gate_in = jnp.clip(0.5 + 1.0 * jax.random.uniform(arg_keys[0], (LENGTH, D), jnp.float32) ** block_scale(arg_keys[0], (LENGTH, D), ((0, 16), (1, 16)), -0.2, 0.2), 0.5, 1.5).astype(jnp.bfloat16)
    key_in = draw_key_in(jax.random.fold_in(arg_keys[6], 71), 0)
    value_in = jnp.clip(0.5 + 1.0 * jax.random.uniform(arg_keys[2], (LENGTH, D), jnp.float32) ** block_scale(arg_keys[2], (LENGTH, D), ((0, 16), (1, 16)), -0.2, 0.2), 0.5, 1.5).astype(jnp.bfloat16)
    filt_in = draw_filt_in(jax.random.fold_in(arg_keys[6], 71), 0)
    skip_gain = centred(arg_keys[4], (D,), 1.0, 3.0, ((0, 16),), jnp.float32)
    running_gram = centred(arg_keys[5], (D, D), 0.3, 2.0, ((0, 16), (1, 16)), jnp.float32)
    return {"gate_in": gate_in, "key_in": key_in, "value_in": value_in, "filt_in": filt_in, "skip_gain": skip_gain, "running_gram": running_gram}


def angle_table(rows, cols, modulus):
    left = jnp.arange(rows, dtype=jnp.int32)
    right = jnp.arange(cols, dtype=jnp.int32)
    turned = (left[:, None] * right[None, :]) % modulus
    angle = turned.astype(jnp.float32) * (2.0 * math.pi / modulus)
    return jnp.cos(angle), jnp.sin(angle)


def batched(form, first, second):
    return jnp.einsum(form, first.astype(jnp.float32), second.astype(jnp.float32), precision=lax.Precision.HIGHEST)


def spectrum(signal, tables):
    c_one, s_one, t_cos, t_sin, c_blk, s_blk = tables
    chans, length = signal.shape
    grid = signal.reshape(chans, length // 128, 128)
    s_re = batched("ka,cab->ckb", c_one, grid)
    s_im = -batched("ka,cab->ckb", s_one, grid)
    t_re = (s_re * t_cos + s_im * t_sin).astype(jnp.bfloat16)
    t_im = (s_im * t_cos - s_re * t_sin).astype(jnp.bfloat16)
    x_re = batched("ckb,bj->ckj", t_re, c_blk) + batched("ckb,bj->ckj", t_im, s_blk)
    x_im = batched("ckb,bj->ckj", t_im, c_blk) - batched("ckb,bj->ckj", t_re, s_blk)
    return x_re, x_im


def inverse(p_re, p_im, tables):
    c_one, s_one, t_cos, t_sin, c_blk, s_blk = tables
    chans = p_re.shape[0]
    width = p_re.shape[1]
    q_re = batched("ckj,jb->ckb", p_re, c_blk) - batched("ckj,jb->ckb", p_im, s_blk)
    q_im = batched("ckj,jb->ckb", p_im, c_blk) + batched("ckj,jb->ckb", p_re, s_blk)
    r_re = (q_re * t_cos - q_im * t_sin).astype(jnp.bfloat16)
    r_im = (q_im * t_cos + q_re * t_sin).astype(jnp.bfloat16)
    result = batched("ka,ckb->cab", c_one, r_re) - batched("ka,ckb->cab", s_one, r_im)
    return (result * (1.0 / (width * 128))).reshape(chans, width * 64)


def reference(gate_in, key_in, value_in, filt_in, skip_gain, running_gram):
    length, width = gate_in.shape
    mixed = (key_in.astype(jnp.float32) * value_in.astype(jnp.float32)).astype(jnp.bfloat16)
    half = length // 128
    c_one, s_one = angle_table(2 * half, half, 2 * half)
    t_cos, t_sin = angle_table(2 * half, 128, 2 * length)
    c_blk, s_blk = angle_table(128, 128, 128)
    tables = (c_one.astype(jnp.bfloat16), s_one.astype(jnp.bfloat16), t_cos, t_sin,
              c_blk.astype(jnp.bfloat16), s_blk.astype(jnp.bfloat16))
    block = 256 if width % 256 == 0 else width
    count = width // block

    def one_block(inputs):
        signal, filt, gates, skips = inputs
        u_re, u_im = spectrum(signal, tables)
        f_re, f_im = spectrum(filt, tables)
        p_re = (u_re * f_re - u_im * f_im).astype(jnp.bfloat16)
        p_im = (u_re * f_im + u_im * f_re).astype(jnp.bfloat16)
        conv = inverse(p_re, p_im, tables)
        mixed_out = (conv + skips[:, None] * signal.astype(jnp.float32)).astype(jnp.bfloat16)
        return (gates.astype(jnp.float32) * mixed_out.astype(jnp.float32)).astype(jnp.bfloat16)

    inputs = (mixed.T.reshape(count, block, length), filt_in.T.reshape(count, block, length),
              gate_in.T.reshape(count, block, length), skip_gain.reshape(count, block))
    gated = lax.map(one_block, inputs).reshape(width, length)
    tokens = length // N_SEQ

    def add_block(index, total):
        start = (index * tokens).astype(jnp.int32)
        rows = lax.dynamic_slice_in_dim(gated, start, tokens, 1)
        term = jnp.dot(rows, rows.T, preferred_element_type=jnp.float32) / length
        return total + term

    summed = lax.fori_loop(0, N_SEQ, add_block, jnp.zeros((width, width), jnp.float32))
    return running_gram + summed
```

```python
import functools
import math

import jax
import jax.numpy as jnp
import numpy as np
from jax import lax
from jax.experimental import pallas as pl
from jax.experimental.pallas import tpu as pltpu
from jax.sharding import PartitionSpec as P

BF = jnp.bfloat16
F32 = jnp.float32
MESH = ("seq", "grp")
VMEM = pl.BlockSpec(memory_space=pltpu.VMEM)
SMEM = pl.BlockSpec(memory_space=pltpu.SMEM)
MIB = 1024 * 1024


def coords(seq, grp):
    return 2 * (seq // 8) + grp // 8, (seq // 2) % 4, seq % 2, grp % 8


def device(x, y, core, z):
    return (8 * (x // 2) + 2 * y + core) * 16 + 8 * (x % 2) + z


def move(array, target):
    pairs = []
    for seq in range(16):
        for grp in range(16):
            pairs.append((16 * seq + grp, device(*target(*coords(seq, grp)))))
    return lax.ppermute(array, MESH, pairs)


def along_x(array, step):
    return move(array, lambda x, y, c, z: ((x + step) % 4, y, c, z))


def along_y(array, step):
    return move(array, lambda x, y, c, z: (x, (y + step) % 4, c, z))


def along_z(array, step):
    return move(array, lambda x, y, c, z: (x, y, c, (z + step) % 8))


def other_core(array):
    return move(array, lambda x, y, c, z: (x, y, 1 - c, z))


def other_x_lo(array):
    return move(array, lambda x, y, c, z: (x ^ 1, y, c, z))


def to_rows(array, first):
    def target(x, y, c, z):
        h, p = x // 2, x % 2
        return 2 * p + (h if first else 1 - h), z // 2, c, 2 * ((y - z // 2) % 4) + (z + h) % 2

    return move(array, target)


def phase(*arrays):
    return lax.optimization_barrier(arrays)


def angles(rows, cols, modulus):
    turned = (np.arange(rows)[:, None] * np.arange(cols)[None, :]) % modulus
    angle = turned.astype(np.float32) * np.float32(2.0 * math.pi / modulus)
    return np.cos(angle), np.sin(angle)


def tables():
    c_one, s_one = angles(128, 64, 128)
    order = np.array([4 * s + q for q in range(4) for s in range(16)])
    c_one, s_one = c_one[:, order], s_one[:, order]
    t_cos, t_sin = angles(128, 128, 16384)
    c_blk, s_blk = angles(128, 128, 128)
    first = np.concatenate([c_one, s_one], 0)
    last = np.concatenate([c_one.T, -s_one.T], 1) / 16384.0
    fwd = np.block([[c_blk, -s_blk], [s_blk, c_blk]])
    bwd = np.block([[c_blk, s_blk], [-s_blk, c_blk]])
    as_bf = [jnp.asarray(t, dtype=F32).astype(BF) for t in (first, last, fwd, bwd)]
    return (*as_bf, jnp.asarray(t_cos, dtype=F32), jnp.asarray(t_sin, dtype=F32))


def prepare_kernel(gate, key, value, filt, out):
    row = lax.broadcasted_iota(jnp.int32, (128, 128), 0)
    col = lax.broadcasted_iota(jnp.int32, (128, 128), 1)
    eye = (row == col).astype(BF)
    mixed = (key[...].astype(F32) * value[...].astype(F32)).astype(BF)
    for place, block in enumerate((mixed, filt[...], gate[...])):
        turned = lax.dot_general(
            eye, block, (((1,), (1,)), ((), ())), preferred_element_type=F32
        ).astype(BF)
        for j in range(4):
            out[j, 32 * place : 32 * place + 32, :] = turned[32 * j : 32 * j + 32, :]


def prepare(gate, key, value, filt):
    block = pl.BlockSpec((512, 128), lambda i: (0, i))
    return pl.pallas_call(
        prepare_kernel,
        grid=(4,),
        in_specs=[block] * 4,
        out_specs=pl.BlockSpec((4, 96, 512), lambda i: (i, 0, 0)),
        out_shape=jax.ShapeDtypeStruct((16, 96, 512), BF),
        name="prepare",
    )(gate, key, value, filt)


GROUP = 8


def conv_kernel(
    where, skip, data, first, last, fwd, bwd, t_cos, t_sin, keep_same, keep_other, send, grid, done
):
    for arr in range(3):
        for half in range(2):
            lo = 32 * arr + 16 * half
            block = data[:, lo : lo + 16, :].astype(F32)
            block = jnp.swapaxes(block, 0, 1).astype(BF)
            for i in range(16):
                for q in range(4):
                    grid[16 * q : 16 * q + 16, (lo + i) * 128 : (lo + i + 1) * 128] = block[
                        i, :, 128 * q : 128 * q + 128
                    ]
    tc = t_cos[...]
    ts = t_sin[...]

    def group(g, carry):
        lanes = pl.ds(pl.multiple_of(g * (GROUP * 128), GROUP * 128), GROUP * 128)
        f_lanes = pl.ds(pl.multiple_of(4096 + g * (GROUP * 128), GROUP * 128), GROUP * 128)
        g_lanes = pl.ds(pl.multiple_of(8192 + g * (GROUP * 128), GROUP * 128), GROUP * 128)
        spectra = []
        for where_lanes in (lanes, f_lanes):
            s = jnp.dot(first[...], grid[:, where_lanes], preferred_element_type=F32)
            rows = []
            for i in range(GROUP):
                s_re = s[:128, 128 * i : 128 * i + 128]
                s_im = -s[128:, 128 * i : 128 * i + 128]
                t_re = (s_re * tc + s_im * ts).astype(BF)
                t_im = (s_im * tc - s_re * ts).astype(BF)
                rows.append(jnp.concatenate([t_re, t_im], 1))
            spectra.append(
                jnp.dot(jnp.concatenate(rows, 0), fwd[...], preferred_element_type=F32)
            )
        u, f = spectra
        u_re, u_im, f_re, f_im = u[:, :128], u[:, 128:], f[:, :128], f[:, 128:]
        p_re = (u_re * f_re - u_im * f_im).astype(BF)
        p_im = (u_re * f_im + u_im * f_re).astype(BF)
        qq = jnp.dot(
            jnp.concatenate([p_re, p_im], 1), bwd[...], preferred_element_type=F32
        )
        cols = []
        for i in range(GROUP):
            q_re = qq[128 * i : 128 * i + 128, :128]
            q_im = qq[128 * i : 128 * i + 128, 128:]
            r_re = (q_re * tc - q_im * ts).astype(BF)
            r_im = (q_im * tc + q_re * ts).astype(BF)
            cols.append(jnp.concatenate([r_re, r_im], 0))
        conv = jnp.dot(last[...], jnp.concatenate(cols, 1), preferred_element_type=F32)
        signal = grid[:, lanes].astype(F32)
        gates = grid[:, g_lanes].astype(F32)
        for i in range(GROUP):
            part = slice(128 * i, 128 * i + 128)
            mixed_out = conv[:, part] + skip[g * GROUP + i] * signal[:, part]
            gated = gates[:, part] * mixed_out.astype(BF).astype(F32)
            done[g * GROUP + i] = gated
        return carry

    lax.fori_loop(0, 32 // GROUP, group, 0)
    core = where[2]
    x_lo = where[0] % 2

    def quarter(lo, part):
        rows = pl.ds(pl.multiple_of(part * 16, 16), 16)
        return jnp.swapaxes(done[lo : lo + 16, rows, :], 0, 1).astype(BF)

    for lo in (0, 16):
        keep_same[:, lo : lo + 16, :] = quarter(lo, 2 * x_lo + core)
        keep_other[:, lo : lo + 16, :] = quarter(lo, 2 * (1 - x_lo) + core)
        send[0, :, lo : lo + 16, :] = quarter(lo, 2 * x_lo + 1 - core)
        send[1, :, lo : lo + 16, :] = quarter(lo, 2 * (1 - x_lo) + 1 - core)


def convolve(where, skips, data):
    piece = jax.ShapeDtypeStruct((16, 32, 128), BF)
    return pl.pallas_call(
        conv_kernel,
        in_specs=[SMEM, SMEM] + [VMEM] * 7,
        out_specs=[VMEM] * 3,
        out_shape=[piece, piece, jax.ShapeDtypeStruct((2, 16, 32, 128), BF)],
        scratch_shapes=[pltpu.VMEM((64, 96 * 128), BF), pltpu.VMEM((32, 64, 128), F32)],
        compiler_params=pltpu.CompilerParams(vmem_limit_bytes=14 * MIB),
        cost_estimate=pl.CostEstimate(
            flops=4 * 10**9, bytes_accessed=3 * 10**6, transcendentals=0
        ),
        name="convolve",
    )(where, skips, data, *tables())


def columns_kernel(where, *refs):
    y, core, first_x, second_x = where[1], where[2], where[4], where[5]
    own, below, above, far_low, far_high, right = refs
    for j, from_x in enumerate((first_x, second_x)):
        for step in (0, -1, 1, 2):
            from_y = (y + step + 4) % 4
            base = 32 * (8 * (from_x // 2) + 2 * from_y)
            for rel in range(2):
                row = pl.ds(pl.multiple_of(base + 32 * ((core + rel) % 2), 32), 32)
                if step == 2:
                    piece = (far_low, far_high)[rel].at[j, 0]
                else:
                    piece = {0: own, -1: below, 1: above}[step].at[j, rel]
                for a in range(16):
                    right[row, 128 * a : 128 * a + 128] = piece[a]


def columns(where, *shards):
    return pl.pallas_call(
        columns_kernel,
        in_specs=[SMEM] + [VMEM] * len(shards),
        out_specs=VMEM,
        out_shape=jax.ShapeDtypeStruct((512, 2048), BF),
        compiler_params=pltpu.CompilerParams(vmem_limit_bytes=12 * MIB),
        cost_estimate=pl.CostEstimate(flops=0, bytes_accessed=4 * 10**6, transcendentals=0),
        name="columns",
    )(where, *shards)


def gram_kernel(steps, n_right, where, *refs):
    rows = 64 * len(steps)
    rights, shard_refs = refs[:n_right], refs[n_right:-3]
    keep, send, left = refs[-3:]
    x, core, z = where[0], where[2], where[3]
    shards = []
    for ref in shard_refs:
        shards += [(ref, j) for j in range(2)] if ref.shape[0] == 2 else [(ref, 0)]
    for n, (ref, j) in enumerate(shards):
        h = (x + n) % 2
        source = (z + steps[n // 2] + 8) % 8
        slot = (source + h + core) % 2
        for rel in range(2):
            row = rows * slot + 64 * (n // 2) + 32 * ((core + rel) % 2)
            row = pl.multiple_of(row, 32)
            for a in range(16):
                left[pl.ds(row, 32), 128 * a : 128 * a + 128] = ref[j, rel, a]
    for half, right in enumerate(rights):
        for sub in range(2):
            lanes = slice(256 * sub, 256 * sub + 256)
            part = lax.dot_general(
                left[...],
                right[lanes, :],
                (((1,), (1,)), ((), ())),
                preferred_element_type=F32,
            )
            keep[half, :, lanes] = part[:rows]
            send[half, :, lanes] = part[rows:]


def gram_part(steps, where, rights, shards):
    rows = 64 * len(steps)
    tile = jax.ShapeDtypeStruct((len(rights), rows, 512), F32)
    return pl.pallas_call(
        functools.partial(gram_kernel, steps, len(rights)),
        in_specs=[SMEM] + [VMEM] * (len(rights) + len(shards)),
        out_specs=[VMEM] * 2,
        out_shape=[tile, tile],
        scratch_shapes=[pltpu.VMEM((2 * rows, 2048), BF)],
        compiler_params=pltpu.CompilerParams(vmem_limit_bytes=14 * MIB),
        cost_estimate=pl.CostEstimate(
            flops=4 * rows * len(rights) * 512 * 2048,
            bytes_accessed=4 * 10**6,
            transcendentals=0,
        ),
        name="gram_part",
    )(where, *rights, *shards)


def finish_kernel(chunks, where, running, *refs):
    out = refs[-1]
    y, core, z = where[1], where[2], where[3]
    for n, steps in enumerate(chunks):
        keep, got, theirs = refs[3 * n : 3 * n + 3]
        for k, step in enumerate(steps):
            source = (z + step + 8) % 8
            h = (source + core) % 2
            from_y = (y + source // 2) % 4
            rows = pl.ds(pl.multiple_of(64 * (4 * h + from_y), 64), 64)
            here = slice(64 * k, 64 * k + 64)
            total = keep[0, here, :] + got[0, here, :] + theirs[here, :]
            out[rows, :] = running[rows, :] + total * (1.0 / 8192.0)


def finish(chunks, where, running, *parts):
    specs = [SMEM, VMEM]
    for steps in chunks:
        half = pl.BlockSpec((1, 64 * len(steps), 512), lambda i: (0, 0, 0))
        specs += [half, half, pl.BlockSpec((64 * len(steps), 512), lambda i: (0, 0))]
    return pl.pallas_call(
        functools.partial(finish_kernel, chunks),
        grid=(1,),
        in_specs=specs,
        out_specs=VMEM,
        out_shape=jax.ShapeDtypeStruct((512, 512), F32),
        compiler_params=pltpu.CompilerParams(vmem_limit_bytes=12 * MIB),
        cost_estimate=pl.CostEstimate(flops=10**6, bytes_accessed=5 * 10**6, transcendentals=0),
        name="finish",
    )(where, running, *parts)


STEPS = (0, -1, 1, -2, 2, -3, 3, 4)
CHUNKS = (STEPS[:5], STEPS[5:])


def local(gate_in, key_in, value_in, filt_in, skip_gain, running_gram):
    seq, grp = lax.axis_index("seq"), lax.axis_index("grp")
    x, y, core, z = coords(seq, grp)
    where = jnp.stack([x, y, core, z, x, x]).astype(jnp.int32)
    across = jnp.stack([x, y, core, z, x, (x + 2) % 4]).astype(jnp.int32)
    beside = jnp.stack([x, y, core, z, (x + 1) % 4, (x + 3) % 4]).astype(jnp.int32)
    skips = lax.dynamic_slice_in_dim(skip_gain, seq * 32, 32, 0)

    outgoing = prepare(gate_in, key_in, value_in, filt_in)
    data = lax.all_to_all(outgoing, "seq", split_axis=0, concat_axis=0, tiled=True)
    same, other, send = convolve(where, skips, data)

    got = other_core(send)
    same = jnp.stack([same, got[0]])
    other = jnp.stack([other, got[1]])
    crossed = (x % 2) != (x // 2)
    row_a = to_rows(jnp.where(crossed, other, same), True)
    row_b = to_rows(jnp.where(crossed, same, other), False)
    below = along_x(other, 1)
    above = along_x(other, 3)
    opposite = along_x(same, 2)

    rows, near, own = phase(
        jnp.stack([row_a, row_b]), jnp.stack([above, below]), jnp.stack([same, opposite])
    )
    ups, downs = [rows], [rows]
    for _ in range(3):
        ups.append(along_z(ups[-1], 1))
        downs.append(along_z(downs[-1], 7))
    far = along_z(ups[3][:1], 1), along_z(downs[3][1:], 7)

    near_up, near_down = along_y(near, 1), along_y(near, 3)
    near_up, near_down, own = phase(near_up, near_down, own)
    near_far = along_y(near_up[:, :1], 1), along_y(near_down[:, 1:], 3)
    own_up, own_down = along_y(own, 1), along_y(own, 3)
    *near_far, own_up, own_down = phase(*near_far, own_up, own_down)
    own_far = along_y(own_up[:, :1], 1), along_y(own_down[:, 1:], 3)
    right = columns(beside, near, near_up, near_down, *near_far)
    own_right = columns(across, own, own_up, own_down, *own_far)

    early = [rows, ups[1], downs[1], ups[2], downs[2]]
    keep, send = gram_part(CHUNKS[0], where, [right], early)
    theirs_a = other_x_lo(keep[0] + other_core(send)[0])
    keep_a, send_a = gram_part(CHUNKS[0], where, [own_right], early)
    got_a = other_core(send_a)

    *far, theirs_a = phase(*far, theirs_a)
    late = [ups[3], downs[3], *far]
    keep_b, send_b = gram_part(CHUNKS[1], where, [own_right, right], late)
    got_b = other_core(send_b)
    theirs_b = other_x_lo(keep_b[1] + got_b[1])
    return finish(
        CHUNKS, where, running_gram, keep_a, got_a, theirs_a, keep_b, got_b, theirs_b
    )


def solution(mesh):
    in_specs = (
        P("seq", "grp"),
        P("seq", "grp"),
        P("seq", "grp"),
        P("seq", "grp"),
        P("grp"),
        P("seq", "grp"),
    )
    out_specs = P("seq", "grp")
    return jax.shard_map(local, mesh=mesh, in_specs=in_specs, out_specs=out_specs, check_vma=False)
```

```python
import functools
import math

import jax
import jax.numpy as jnp
import numpy as np
from jax import lax
from jax.experimental import pallas as pl
from jax.experimental.pallas import tpu as pltpu
from jax.sharding import PartitionSpec as P

BF = jnp.bfloat16
F32 = jnp.float32
MESH = ("seq", "grp")
VMEM = pl.BlockSpec(memory_space=pltpu.VMEM)
SMEM = pl.BlockSpec(memory_space=pltpu.SMEM)
ANY = pl.BlockSpec(memory_space=pl.ANY)
MIB = 1024 * 1024


def coords(seq, grp):
    return 2 * (seq // 8) + grp // 8, (seq // 2) % 4, seq % 2, grp % 8


def device(x, y, core, z):
    return (8 * (x // 2) + 2 * y + core) * 16 + 8 * (x % 2) + z


def move(array, target):
    pairs = []
    for seq in range(16):
        for grp in range(16):
            pairs.append((16 * seq + grp, device(*target(*coords(seq, grp)))))
    return lax.ppermute(array, MESH, pairs)


def along_x(array, step):
    return move(array, lambda x, y, c, z: ((x + step) % 4, y, c, z))


def along_y(array, step):
    return move(array, lambda x, y, c, z: (x, (y + step) % 4, c, z))


def along_z(array, step):
    return move(array, lambda x, y, c, z: (x, y, c, (z + step) % 8))


def other_core(array):
    return move(array, lambda x, y, c, z: (x, y, 1 - c, z))


def other_x_lo(array):
    return move(array, lambda x, y, c, z: (x ^ 1, y, c, z))


def to_rows(array, first):
    def target(x, y, c, z):
        h, p = x // 2, x % 2
        return 2 * p + (h if first else 1 - h), z // 2, c, 2 * ((y - z // 2) % 4) + (z + h) % 2

    return move(array, target)


def after_kernel(n_after, *refs):
    sources, targets = refs[: len(refs) - n_after], refs[len(refs) - n_after :]
    n = 0
    for target in targets:
        for place in range(target.shape[0]):
            target[place] = sources[n][...]
            n += 1


def after(stacks, *earlier):
    pieces = [piece for stack in stacks for piece in stack]
    shapes = [jax.ShapeDtypeStruct((len(stack), *stack[0].shape), BF) for stack in stacks]
    return pl.pallas_call(
        lambda *refs: after_kernel(
            len(stacks), *refs[: len(pieces)], *refs[len(pieces) + len(earlier) :]
        ),
        in_specs=[VMEM] * len(pieces) + [ANY] * len(earlier),
        out_specs=[VMEM] * len(stacks),
        out_shape=shapes,
        compiler_params=pltpu.CompilerParams(vmem_limit_bytes=8 * MIB),
        cost_estimate=pl.CostEstimate(flops=0, bytes_accessed=10**6, transcendentals=0),
        name="after",
    )(*pieces, *earlier)


def angles(rows, cols, modulus):
    turned = (np.arange(rows)[:, None] * np.arange(cols)[None, :]) % modulus
    angle = turned.astype(np.float32) * np.float32(2.0 * math.pi / modulus)
    return np.cos(angle), np.sin(angle)


def tables():
    c_one, s_one = angles(128, 64, 128)
    order = np.array([4 * s + q for q in range(4) for s in range(16)])
    c_one, s_one = c_one[:, order], s_one[:, order]
    t_cos, t_sin = angles(128, 128, 16384)
    c_blk, s_blk = angles(128, 128, 128)
    first = np.concatenate([c_one, s_one], 0)
    last = np.concatenate([c_one.T, -s_one.T], 1) / 16384.0
    fwd = np.block([[c_blk, -s_blk], [s_blk, c_blk]])
    bwd = np.block([[c_blk, s_blk], [-s_blk, c_blk]])
    as_bf = [jnp.asarray(t, dtype=F32).astype(BF) for t in (first, last, fwd, bwd)]
    return (*as_bf, jnp.asarray(t_cos, dtype=F32), jnp.asarray(t_sin, dtype=F32))


def prepare_kernel(gate, key, value, filt, out):
    row = lax.broadcasted_iota(jnp.int32, (128, 128), 0)
    col = lax.broadcasted_iota(jnp.int32, (128, 128), 1)
    eye = (row == col).astype(BF)
    mixed = (key[...].astype(F32) * value[...].astype(F32)).astype(BF)
    for place, block in enumerate((mixed, filt[...], gate[...])):
        turned = lax.dot_general(
            eye, block, (((1,), (1,)), ((), ())), preferred_element_type=F32
        ).astype(BF)
        for j in range(4):
            out[j, 32 * place : 32 * place + 32, :] = turned[32 * j : 32 * j + 32, :]


def prepare(gate, key, value, filt):
    block = pl.BlockSpec((512, 128), lambda i: (0, i))
    return pl.pallas_call(
        prepare_kernel,
        grid=(4,),
        in_specs=[block] * 4,
        out_specs=pl.BlockSpec((4, 96, 512), lambda i: (i, 0, 0)),
        out_shape=jax.ShapeDtypeStruct((16, 96, 512), BF),
        name="prepare",
    )(gate, key, value, filt)


GROUP = 8


def conv_kernel(
    where, skip, data, first, last, fwd, bwd, t_cos, t_sin, keep_same, keep_other, send, grid, done
):
    for arr in range(3):
        for half in range(2):
            lo = 32 * arr + 16 * half
            block = data[:, lo : lo + 16, :].astype(F32)
            block = jnp.swapaxes(block, 0, 1).astype(BF)
            for i in range(16):
                for q in range(4):
                    grid[16 * q : 16 * q + 16, (lo + i) * 128 : (lo + i + 1) * 128] = block[
                        i, :, 128 * q : 128 * q + 128
                    ]
    tc = t_cos[...]
    ts = t_sin[...]

    def group(g, carry):
        lanes = pl.ds(pl.multiple_of(g * (GROUP * 128), GROUP * 128), GROUP * 128)
        f_lanes = pl.ds(pl.multiple_of(4096 + g * (GROUP * 128), GROUP * 128), GROUP * 128)
        g_lanes = pl.ds(pl.multiple_of(8192 + g * (GROUP * 128), GROUP * 128), GROUP * 128)
        spectra = []
        for where_lanes in (lanes, f_lanes):
            s = jnp.dot(first[...], grid[:, where_lanes], preferred_element_type=F32)
            rows = []
            for i in range(GROUP):
                s_re = s[:128, 128 * i : 128 * i + 128]
                s_im = -s[128:, 128 * i : 128 * i + 128]
                t_re = (s_re * tc + s_im * ts).astype(BF)
                t_im = (s_im * tc - s_re * ts).astype(BF)
                rows.append(jnp.concatenate([t_re, t_im], 1))
            spectra.append(
                jnp.dot(jnp.concatenate(rows, 0), fwd[...], preferred_element_type=F32)
            )
        u, f = spectra
        u_re, u_im, f_re, f_im = u[:, :128], u[:, 128:], f[:, :128], f[:, 128:]
        p_re = (u_re * f_re - u_im * f_im).astype(BF)
        p_im = (u_re * f_im + u_im * f_re).astype(BF)
        qq = jnp.dot(
            jnp.concatenate([p_re, p_im], 1), bwd[...], preferred_element_type=F32
        )
        cols = []
        for i in range(GROUP):
            q_re = qq[128 * i : 128 * i + 128, :128]
            q_im = qq[128 * i : 128 * i + 128, 128:]
            r_re = (q_re * tc - q_im * ts).astype(BF)
            r_im = (q_im * tc + q_re * ts).astype(BF)
            cols.append(jnp.concatenate([r_re, r_im], 0))
        conv = jnp.dot(last[...], jnp.concatenate(cols, 1), preferred_element_type=F32)
        signal = grid[:, lanes].astype(F32)
        gates = grid[:, g_lanes].astype(F32)
        for i in range(GROUP):
            part = slice(128 * i, 128 * i + 128)
            mixed_out = conv[:, part] + skip[g * GROUP + i] * signal[:, part]
            gated = gates[:, part] * mixed_out.astype(BF).astype(F32)
            done[g * GROUP + i] = gated
        return carry

    lax.fori_loop(0, 32 // GROUP, group, 0)
    core = where[2]
    x_lo = where[0] % 2

    def quarter(lo, part):
        rows = pl.ds(pl.multiple_of(part * 16, 16), 16)
        return jnp.swapaxes(done[lo : lo + 16, rows, :], 0, 1).astype(BF)

    for lo in (0, 16):
        keep_same[:, lo : lo + 16, :] = quarter(lo, 2 * x_lo + core)
        keep_other[:, lo : lo + 16, :] = quarter(lo, 2 * (1 - x_lo) + core)
        send[0, :, lo : lo + 16, :] = quarter(lo, 2 * x_lo + 1 - core)
        send[1, :, lo : lo + 16, :] = quarter(lo, 2 * (1 - x_lo) + 1 - core)


def convolve(where, skips, data):
    piece = jax.ShapeDtypeStruct((16, 32, 128), BF)
    return pl.pallas_call(
        conv_kernel,
        in_specs=[SMEM, SMEM] + [VMEM] * 7,
        out_specs=[VMEM] * 3,
        out_shape=[piece, piece, jax.ShapeDtypeStruct((2, 16, 32, 128), BF)],
        scratch_shapes=[pltpu.VMEM((64, 96 * 128), BF), pltpu.VMEM((32, 64, 128), F32)],
        compiler_params=pltpu.CompilerParams(vmem_limit_bytes=14 * MIB),
        cost_estimate=pl.CostEstimate(
            flops=4 * 10**9, bytes_accessed=3 * 10**6, transcendentals=0
        ),
        name="convolve",
    )(where, skips, data, *tables())


def columns_kernel(where, *refs):
    y, core, first_x, second_x = where[1], where[2], where[4], where[5]
    own, below, above, far_low, far_high = refs[:5]
    right = refs[-1]
    for j, from_x in enumerate((first_x, second_x)):
        for step in (0, -1, 1, 2):
            from_y = (y + step + 4) % 4
            base = 32 * (8 * (from_x // 2) + 2 * from_y)
            for rel in range(2):
                row = pl.ds(pl.multiple_of(base + 32 * ((core + rel) % 2), 32), 32)
                if step == 2:
                    piece = (far_low, far_high)[rel].at[j, 0]
                else:
                    piece = {0: own, -1: below, 1: above}[step].at[j, rel]
                for a in range(16):
                    right[row, 128 * a : 128 * a + 128] = piece[a]


def columns(where, shards, *earlier):
    return pl.pallas_call(
        columns_kernel,
        in_specs=[SMEM] + [VMEM] * len(shards) + [ANY] * len(earlier),
        out_specs=VMEM,
        out_shape=jax.ShapeDtypeStruct((512, 2048), BF),
        compiler_params=pltpu.CompilerParams(vmem_limit_bytes=12 * MIB),
        cost_estimate=pl.CostEstimate(flops=0, bytes_accessed=4 * 10**6, transcendentals=0),
        name="columns",
    )(where, *shards, *earlier)


def gram_kernel(steps, n_right, n_earlier, where, *refs):
    rows = 64 * len(steps)
    rights, shard_refs = refs[:n_right], refs[n_right : -3 - n_earlier]
    keep, send, left = refs[-3:]
    x, core, z = where[0], where[2], where[3]
    shards = []
    for ref in shard_refs:
        shards += [(ref, j) for j in range(2)] if ref.shape[0] == 2 else [(ref, 0)]
    for n, (ref, j) in enumerate(shards):
        h = (x + n) % 2
        source = (z + steps[n // 2] + 8) % 8
        slot = (source + h + core) % 2
        for rel in range(2):
            row = rows * slot + 64 * (n // 2) + 32 * ((core + rel) % 2)
            row = pl.multiple_of(row, 32)
            for a in range(16):
                left[pl.ds(row, 32), 128 * a : 128 * a + 128] = ref[j, rel, a]
    for half, right in enumerate(rights):
        for sub in range(2):
            lanes = slice(256 * sub, 256 * sub + 256)
            part = lax.dot_general(
                left[...],
                right[lanes, :],
                (((1,), (1,)), ((), ())),
                preferred_element_type=F32,
            )
            keep[half, :, lanes] = part[:rows]
            send[half, :, lanes] = part[rows:]


def gram_part(steps, where, rights, shards, *earlier):
    rows = 64 * len(steps)
    tile = jax.ShapeDtypeStruct((len(rights), rows, 512), F32)
    return pl.pallas_call(
        functools.partial(gram_kernel, steps, len(rights), len(earlier)),
        in_specs=[SMEM] + [VMEM] * (len(rights) + len(shards)) + [ANY] * len(earlier),
        out_specs=[VMEM] * 2,
        out_shape=[tile, tile],
        scratch_shapes=[pltpu.VMEM((2 * rows, 2048), BF)],
        compiler_params=pltpu.CompilerParams(vmem_limit_bytes=14 * MIB),
        cost_estimate=pl.CostEstimate(
            flops=4 * rows * len(rights) * 512 * 2048,
            bytes_accessed=4 * 10**6,
            transcendentals=0,
        ),
        name="gram_part",
    )(where, *rights, *shards, *earlier)


def finish_kernel(chunks, where, running, *refs):
    out = refs[-1]
    y, core, z = where[1], where[2], where[3]
    for n, steps in enumerate(chunks):
        keep, got, theirs = refs[3 * n : 3 * n + 3]
        for k, step in enumerate(steps):
            source = (z + step + 8) % 8
            h = (source + core) % 2
            from_y = (y + source // 2) % 4
            rows = pl.ds(pl.multiple_of(64 * (4 * h + from_y), 64), 64)
            here = slice(64 * k, 64 * k + 64)
            total = keep[0, here, :] + got[0, here, :] + theirs[here, :]
            out[rows, :] = running[rows, :] + total * (1.0 / 8192.0)


def finish(chunks, where, running, *parts):
    specs = [SMEM, VMEM]
    for steps in chunks:
        half = pl.BlockSpec((1, 64 * len(steps), 512), lambda i: (0, 0, 0))
        specs += [half, half, pl.BlockSpec((64 * len(steps), 512), lambda i: (0, 0))]
    return pl.pallas_call(
        functools.partial(finish_kernel, chunks),
        grid=(1,),
        in_specs=specs,
        out_specs=VMEM,
        out_shape=jax.ShapeDtypeStruct((512, 512), F32),
        compiler_params=pltpu.CompilerParams(vmem_limit_bytes=12 * MIB),
        cost_estimate=pl.CostEstimate(flops=10**6, bytes_accessed=5 * 10**6, transcendentals=0),
        name="finish",
    )(where, running, *parts)


STEPS = (0, -1, 1, -2, 2, -3, 3, 4)
CHUNKS = (STEPS[:5], STEPS[5:])


def local(gate_in, key_in, value_in, filt_in, skip_gain, running_gram):
    seq, grp = lax.axis_index("seq"), lax.axis_index("grp")
    x, y, core, z = coords(seq, grp)
    where = jnp.stack([x, y, core, z, x, x]).astype(jnp.int32)
    across = jnp.stack([x, y, core, z, x, (x + 2) % 4]).astype(jnp.int32)
    beside = jnp.stack([x, y, core, z, (x + 1) % 4, (x + 3) % 4]).astype(jnp.int32)
    skips = lax.dynamic_slice_in_dim(skip_gain, seq * 32, 32, 0)

    outgoing = prepare(gate_in, key_in, value_in, filt_in)
    data = lax.all_to_all(outgoing, "seq", split_axis=0, concat_axis=0, tiled=True)
    same, other, send = convolve(where, skips, data)

    got = other_core(send)
    same = jnp.stack([same, got[0]])
    other = jnp.stack([other, got[1]])
    crossed = (x % 2) != (x // 2)
    row_a = to_rows(jnp.where(crossed, other, same), True)
    row_b = to_rows(jnp.where(crossed, same, other), False)
    below = along_x(other, 1)
    above = along_x(other, 3)
    opposite = along_x(same, 2)

    rows, near = after([[row_a, row_b], [above, below]], same, opposite)
    ups, downs = [rows], [rows]
    for _ in range(3):
        ups.append(along_z(ups[-1], 1))
        downs.append(along_z(downs[-1], 7))
    far = along_z(ups[3][:1], 1), along_z(downs[3][1:], 7)

    near_up, near_down = along_y(near, 1), along_y(near, 3)
    (own,) = after([[same, opposite]], near_up, near_down)
    near_far = along_y(near_up[:, :1], 1), along_y(near_down[:, 1:], 3)
    own_up, own_down = along_y(own, 1), along_y(own, 3)
    right = columns(beside, [near, near_up, near_down, *near_far], own_up, own_down)
    own_far = along_y(own_up[:, :1], 1), along_y(own_down[:, 1:], 3)
    own_right = columns(across, [own, own_up, own_down, *own_far])

    early = [rows, ups[1], downs[1], ups[2], downs[2]]
    keep, send = gram_part(CHUNKS[0], where, [right], early)
    theirs_a = other_x_lo(keep[0] + other_core(send)[0])
    keep_a, send_a = gram_part(CHUNKS[0], where, [own_right], early)
    got_a = other_core(send_a)

    late = [ups[3], downs[3], *far]
    keep_b, send_b = gram_part(CHUNKS[1], where, [own_right, right], late, theirs_a, keep_a)
    got_b = other_core(send_b)
    theirs_b = other_x_lo(keep_b[1] + got_b[1])
    return finish(
        CHUNKS, where, running_gram, keep_a, got_a, theirs_a, keep_b, got_b, theirs_b
    )


def solution(mesh):
    in_specs = (
        P("seq", "grp"),
        P("seq", "grp"),
        P("seq", "grp"),
        P("seq", "grp"),
        P("grp"),
        P("seq", "grp"),
    )
    out_specs = P("seq", "grp")
    return jax.shard_map(local, mesh=mesh, in_specs=in_specs, out_specs=out_specs, check_vma=False)
```

```python
import functools
import math

import jax
import jax.numpy as jnp
import numpy as np
from jax import lax
from jax.experimental import pallas as pl
from jax.experimental.pallas import tpu as pltpu
from jax.sharding import PartitionSpec as P

BF = jnp.bfloat16
F32 = jnp.float32
MESH = ("seq", "grp")
VMEM = pl.BlockSpec(memory_space=pltpu.VMEM)
SMEM = pl.BlockSpec(memory_space=pltpu.SMEM)
ANY = pl.BlockSpec(memory_space=pl.ANY)
MIB = 1024 * 1024


def coords(seq, grp):
    return 2 * (seq // 8) + grp // 8, (seq // 2) % 4, seq % 2, grp % 8


def device(x, y, core, z):
    return (8 * (x // 2) + 2 * y + core) * 16 + 8 * (x % 2) + z


def move(array, target):
    pairs = []
    for seq in range(16):
        for grp in range(16):
            pairs.append((16 * seq + grp, device(*target(*coords(seq, grp)))))
    return lax.ppermute(array, MESH, pairs)


def along_x(array, step):
    return move(array, lambda x, y, c, z: ((x + step) % 4, y, c, z))


def along_y(array, step):
    return move(array, lambda x, y, c, z: (x, (y + step) % 4, c, z))


def along_z(array, step):
    return move(array, lambda x, y, c, z: (x, y, c, (z + step) % 8))


def other_core(array):
    return move(array, lambda x, y, c, z: (x, y, 1 - c, z))


def other_x_lo(array):
    return move(array, lambda x, y, c, z: (x ^ 1, y, c, z))


def to_rows(array, first):
    def target(x, y, c, z):
        h, p = x // 2, x % 2
        return 2 * p + (h if first else 1 - h), z // 2, c, 2 * ((y - z // 2) % 4) + (z + h) % 2

    return move(array, target)


def after_kernel(n_after, *refs):
    sources, targets = refs[: len(refs) - n_after], refs[len(refs) - n_after :]
    n = 0
    for target in targets:
        for place in range(target.shape[0]):
            target[place] = sources[n][...]
            n += 1


def after(stacks, *earlier):
    pieces = [piece for stack in stacks for piece in stack]
    shapes = [jax.ShapeDtypeStruct((len(stack), *stack[0].shape), BF) for stack in stacks]
    return pl.pallas_call(
        lambda *refs: after_kernel(
            len(stacks), *refs[: len(pieces)], *refs[len(pieces) + len(earlier) :]
        ),
        in_specs=[VMEM] * len(pieces) + [ANY] * len(earlier),
        out_specs=[VMEM] * len(stacks),
        out_shape=shapes,
        compiler_params=pltpu.CompilerParams(vmem_limit_bytes=8 * MIB),
        cost_estimate=pl.CostEstimate(flops=0, bytes_accessed=10**6, transcendentals=0),
        name="after",
    )(*pieces, *earlier)


def angles(rows, cols, modulus):
    turned = (np.arange(rows)[:, None] * np.arange(cols)[None, :]) % modulus
    angle = turned.astype(np.float32) * np.float32(2.0 * math.pi / modulus)
    return np.cos(angle), np.sin(angle)


def tables():
    c_one, s_one = angles(128, 64, 128)
    order = np.array([4 * s + q for q in range(4) for s in range(16)])
    c_one, s_one = c_one[:, order], s_one[:, order]
    t_cos, t_sin = angles(128, 128, 16384)
    c_blk, s_blk = angles(128, 128, 128)
    first = np.concatenate([c_one, s_one], 0)
    last = np.concatenate([c_one.T, -s_one.T], 1) / 16384.0
    fwd = np.block([[c_blk, -s_blk], [s_blk, c_blk]])
    bwd = np.block([[c_blk, s_blk], [-s_blk, c_blk]])
    as_bf = [jnp.asarray(t, dtype=F32).astype(BF) for t in (first, last, fwd, bwd)]
    return (*as_bf, jnp.asarray(t_cos, dtype=F32), jnp.asarray(t_sin, dtype=F32))


def prepare_kernel(gate, key, value, filt, out):
    row = lax.broadcasted_iota(jnp.int32, (128, 128), 0)
    col = lax.broadcasted_iota(jnp.int32, (128, 128), 1)
    eye = (row == col).astype(BF)
    mixed = (key[...].astype(F32) * value[...].astype(F32)).astype(BF)
    for place, block in enumerate((mixed, filt[...], gate[...])):
        turned = lax.dot_general(
            eye, block, (((1,), (1,)), ((), ())), preferred_element_type=F32
        ).astype(BF)
        for j in range(4):
            out[j, 32 * place : 32 * place + 32, :] = turned[32 * j : 32 * j + 32, :]


def prepare(gate, key, value, filt):
    block = pl.BlockSpec((512, 128), lambda i: (0, i))
    return pl.pallas_call(
        prepare_kernel,
        grid=(4,),
        in_specs=[block] * 4,
        out_specs=pl.BlockSpec((4, 96, 512), lambda i: (i, 0, 0)),
        out_shape=jax.ShapeDtypeStruct((16, 96, 512), BF),
        name="prepare",
    )(gate, key, value, filt)


GROUP = 8


def conv_kernel(
    where, skip, data, first, last, fwd, bwd, t_cos, t_sin, keep_same, keep_other, send, grid, done
):
    for arr in range(3):
        for half in range(2):
            lo = 32 * arr + 16 * half
            block = data[:, lo : lo + 16, :].astype(F32)
            block = jnp.swapaxes(block, 0, 1).astype(BF)
            for i in range(16):
                for q in range(4):
                    grid[16 * q : 16 * q + 16, (lo + i) * 128 : (lo + i + 1) * 128] = block[
                        i, :, 128 * q : 128 * q + 128
                    ]
    tc = t_cos[...]
    ts = t_sin[...]

    def group(g, carry):
        lanes = pl.ds(pl.multiple_of(g * (GROUP * 128), GROUP * 128), GROUP * 128)
        f_lanes = pl.ds(pl.multiple_of(4096 + g * (GROUP * 128), GROUP * 128), GROUP * 128)
        g_lanes = pl.ds(pl.multiple_of(8192 + g * (GROUP * 128), GROUP * 128), GROUP * 128)
        spectra = []
        for where_lanes in (lanes, f_lanes):
            s = jnp.dot(first[...], grid[:, where_lanes], preferred_element_type=F32)
            rows = []
            for i in range(GROUP):
                s_re = s[:128, 128 * i : 128 * i + 128]
                s_im = -s[128:, 128 * i : 128 * i + 128]
                t_re = (s_re * tc + s_im * ts).astype(BF)
                t_im = (s_im * tc - s_re * ts).astype(BF)
                rows.append(jnp.concatenate([t_re, t_im], 1))
            spectra.append(
                jnp.dot(jnp.concatenate(rows, 0), fwd[...], preferred_element_type=F32)
            )
        u, f = spectra
        u_re, u_im, f_re, f_im = u[:, :128], u[:, 128:], f[:, :128], f[:, 128:]
        p_re = (u_re * f_re - u_im * f_im).astype(BF)
        p_im = (u_re * f_im + u_im * f_re).astype(BF)
        qq = jnp.dot(
            jnp.concatenate([p_re, p_im], 1), bwd[...], preferred_element_type=F32
        )
        cols = []
        for i in range(GROUP):
            q_re = qq[128 * i : 128 * i + 128, :128]
            q_im = qq[128 * i : 128 * i + 128, 128:]
            r_re = (q_re * tc - q_im * ts).astype(BF)
            r_im = (q_im * tc + q_re * ts).astype(BF)
            cols.append(jnp.concatenate([r_re, r_im], 0))
        conv = jnp.dot(last[...], jnp.concatenate(cols, 1), preferred_element_type=F32)
        signal = grid[:, lanes].astype(F32)
        gates = grid[:, g_lanes].astype(F32)
        for i in range(GROUP):
            part = slice(128 * i, 128 * i + 128)
            mixed_out = conv[:, part] + skip[g * GROUP + i] * signal[:, part]
            gated = gates[:, part] * mixed_out.astype(BF).astype(F32)
            done[g * GROUP + i] = gated
        return carry

    lax.fori_loop(0, 32 // GROUP, group, 0)
    core = where[2]
    x_lo = where[0] % 2

    def quarter(lo, part):
        rows = pl.ds(pl.multiple_of(part * 16, 16), 16)
        return jnp.swapaxes(done[lo : lo + 16, rows, :], 0, 1).astype(BF)

    for lo in (0, 16):
        keep_same[:, lo : lo + 16, :] = quarter(lo, 2 * x_lo + core)
        keep_other[:, lo : lo + 16, :] = quarter(lo, 2 * (1 - x_lo) + core)
        send[0, :, lo : lo + 16, :] = quarter(lo, 2 * x_lo + 1 - core)
        send[1, :, lo : lo + 16, :] = quarter(lo, 2 * (1 - x_lo) + 1 - core)


def convolve(where, skips, data):
    piece = jax.ShapeDtypeStruct((16, 32, 128), BF)
    return pl.pallas_call(
        conv_kernel,
        in_specs=[SMEM, SMEM] + [VMEM] * 7,
        out_specs=[VMEM] * 3,
        out_shape=[piece, piece, jax.ShapeDtypeStruct((2, 16, 32, 128), BF)],
        scratch_shapes=[pltpu.VMEM((64, 96 * 128), BF), pltpu.VMEM((32, 64, 128), F32)],
        compiler_params=pltpu.CompilerParams(vmem_limit_bytes=14 * MIB),
        cost_estimate=pl.CostEstimate(
            flops=4 * 10**9, bytes_accessed=3 * 10**6, transcendentals=0
        ),
        name="convolve",
    )(where, skips, data, *tables())


def columns_kernel(where, *refs):
    y, core, first_x, second_x = where[1], where[2], where[4], where[5]
    own, below, above, far_low, far_high = refs[:5]
    right = refs[-1]
    for j, from_x in enumerate((first_x, second_x)):
        for step in (0, -1, 1, 2):
            from_y = (y + step + 4) % 4
            base = 32 * (8 * (from_x // 2) + 2 * from_y)
            for rel in range(2):
                row = pl.ds(pl.multiple_of(base + 32 * ((core + rel) % 2), 32), 32)
                if step == 2:
                    piece = (far_low, far_high)[rel].at[j, 0]
                else:
                    piece = {0: own, -1: below, 1: above}[step].at[j, rel]
                for a in range(16):
                    right[row, 128 * a : 128 * a + 128] = piece[a]


def columns(where, shards, *earlier):
    return pl.pallas_call(
        columns_kernel,
        in_specs=[SMEM] + [VMEM] * len(shards) + [ANY] * len(earlier),
        out_specs=VMEM,
        out_shape=jax.ShapeDtypeStruct((512, 2048), BF),
        compiler_params=pltpu.CompilerParams(vmem_limit_bytes=12 * MIB),
        cost_estimate=pl.CostEstimate(flops=0, bytes_accessed=4 * 10**6, transcendentals=0),
        name="columns",
    )(where, *shards, *earlier)


def gram_kernel(steps, n_right, n_earlier, where, *refs):
    rows = 64 * len(steps)
    rights, shard_refs = refs[:n_right], refs[n_right : -3 - n_earlier]
    keep, send, left = refs[-3:]
    x, core, z = where[0], where[2], where[3]
    shards = []
    for ref in shard_refs:
        shards += [(ref, j) for j in range(2)] if ref.shape[0] == 2 else [(ref, 0)]
    for n, (ref, j) in enumerate(shards):
        h = (x + n) % 2
        source = (z + steps[n // 2] + 8) % 8
        slot = (source + h + core) % 2
        for rel in range(2):
            row = rows * slot + 64 * (n // 2) + 32 * ((core + rel) % 2)
            row = pl.multiple_of(row, 32)
            for a in range(16):
                left[pl.ds(row, 32), 128 * a : 128 * a + 128] = ref[j, rel, a]
    for half, right in enumerate(rights):
        for sub in range(2):
            lanes = slice(256 * sub, 256 * sub + 256)
            part = lax.dot_general(
                left[...],
                right[lanes, :],
                (((1,), (1,)), ((), ())),
                preferred_element_type=F32,
            )
            keep[half, :, lanes] = part[:rows]
            send[half, :, lanes] = part[rows:]


def gram_part(steps, where, rights, shards, *earlier):
    rows = 64 * len(steps)
    tile = jax.ShapeDtypeStruct((len(rights), rows, 512), F32)
    return pl.pallas_call(
        functools.partial(gram_kernel, steps, len(rights), len(earlier)),
        in_specs=[SMEM] + [VMEM] * (len(rights) + len(shards)) + [ANY] * len(earlier),
        out_specs=[VMEM] * 2,
        out_shape=[tile, tile],
        scratch_shapes=[pltpu.VMEM((2 * rows, 2048), BF)],
        compiler_params=pltpu.CompilerParams(vmem_limit_bytes=14 * MIB),
        cost_estimate=pl.CostEstimate(
            flops=4 * rows * len(rights) * 512 * 2048,
            bytes_accessed=4 * 10**6,
            transcendentals=0,
        ),
        name="gram_part",
    )(where, *rights, *shards, *earlier)


def finish_kernel(chunks, where, running, *refs):
    out = refs[-1]
    y, core, z = where[1], where[2], where[3]
    for n, steps in enumerate(chunks):
        keep, got, theirs = refs[3 * n : 3 * n + 3]
        for k, step in enumerate(steps):
            source = (z + step + 8) % 8
            h = (source + core) % 2
            from_y = (y + source // 2) % 4
            rows = pl.ds(pl.multiple_of(64 * (4 * h + from_y), 64), 64)
            here = slice(64 * k, 64 * k + 64)
            total = keep[0, here, :] + got[0, here, :] + theirs[here, :]
            out[rows, :] = running[rows, :] + total * (1.0 / 8192.0)


def finish(chunks, where, running, *parts):
    specs = [SMEM, VMEM]
    for steps in chunks:
        half = pl.BlockSpec((1, 64 * len(steps), 512), lambda i: (0, 0, 0))
        specs += [half, half, pl.BlockSpec((64 * len(steps), 512), lambda i: (0, 0))]
    return pl.pallas_call(
        functools.partial(finish_kernel, chunks),
        grid=(1,),
        in_specs=specs,
        out_specs=VMEM,
        out_shape=jax.ShapeDtypeStruct((512, 512), F32),
        compiler_params=pltpu.CompilerParams(vmem_limit_bytes=12 * MIB),
        cost_estimate=pl.CostEstimate(flops=10**6, bytes_accessed=5 * 10**6, transcendentals=0),
        name="finish",
    )(where, running, *parts)


STEPS = (0, -1, 1, -2, 2, -3, 3, 4)
CHUNKS = (STEPS[:7], STEPS[7:])


def local(gate_in, key_in, value_in, filt_in, skip_gain, running_gram):
    seq, grp = lax.axis_index("seq"), lax.axis_index("grp")
    x, y, core, z = coords(seq, grp)
    where = jnp.stack([x, y, core, z, x, x]).astype(jnp.int32)
    across = jnp.stack([x, y, core, z, x, (x + 2) % 4]).astype(jnp.int32)
    beside = jnp.stack([x, y, core, z, (x + 1) % 4, (x + 3) % 4]).astype(jnp.int32)
    skips = lax.dynamic_slice_in_dim(skip_gain, seq * 32, 32, 0)

    outgoing = prepare(gate_in, key_in, value_in, filt_in)
    data = lax.all_to_all(outgoing, "seq", split_axis=0, concat_axis=0, tiled=True)
    same, other, send = convolve(where, skips, data)

    got = other_core(send)
    same = jnp.stack([same, got[0]])
    other = jnp.stack([other, got[1]])
    crossed = (x % 2) != (x // 2)
    row_a = to_rows(jnp.where(crossed, other, same), True)
    row_b = to_rows(jnp.where(crossed, same, other), False)
    below = along_x(other, 1)
    above = along_x(other, 3)
    opposite = along_x(same, 2)

    rows, near = after([[row_a, row_b], [above, below]], same, opposite)
    ups, downs = [rows], [rows]
    for _ in range(3):
        ups.append(along_z(ups[-1], 1))
        downs.append(along_z(downs[-1], 7))
    far = along_z(ups[3][:1], 1), along_z(downs[3][1:], 7)

    near_up, near_down = along_y(near, 1), along_y(near, 3)
    (own,) = after([[same, opposite]], near_up, near_down)
    near_far = along_y(near_up[:, :1], 1), along_y(near_down[:, 1:], 3)
    own_up, own_down = along_y(own, 1), along_y(own, 3)
    right = columns(beside, [near, near_up, near_down, *near_far])
    own_far = along_y(own_up[:, :1], 1), along_y(own_down[:, 1:], 3)
    own_right = columns(across, [own, own_up, own_down, *own_far])

    early = [rows, ups[1], downs[1], ups[2], downs[2], ups[3], downs[3]]
    keep, send = gram_part(CHUNKS[0], where, [right], early, own_right)
    half_a = keep[0] + other_core(send)[0]
    theirs_a = other_x_lo(half_a)
    keep_a, send_a = gram_part(CHUNKS[0], where, [own_right], early, keep)
    got_a = other_core(send_a)

    late = [*far]
    keep_b, send_b = gram_part(CHUNKS[1], where, [own_right, right], late)
    got_b = other_core(send_b)
    theirs_b = other_x_lo(keep_b[1] + got_b[1])
    return finish(
        CHUNKS, where, running_gram, keep_a, got_a, theirs_a, keep_b, got_b, theirs_b
    )


def solution(mesh):
    in_specs = (
        P("seq", "grp"),
        P("seq", "grp"),
        P("seq", "grp"),
        P("seq", "grp"),
        P("grp"),
        P("seq", "grp"),
    )
    out_specs = P("seq", "grp")
    return jax.shard_map(local, mesh=mesh, in_specs=in_specs, out_specs=out_specs, check_vma=False)
```

```python
import functools
import math

import jax
import jax.numpy as jnp
import numpy as np
from jax import lax
from jax.experimental import pallas as pl
from jax.experimental.pallas import tpu as pltpu
from jax.sharding import PartitionSpec as P

BF = jnp.bfloat16
F32 = jnp.float32
MESH = ("seq", "grp")
VMEM = pl.BlockSpec(memory_space=pltpu.VMEM)
SMEM = pl.BlockSpec(memory_space=pltpu.SMEM)
MIB = 1024 * 1024


def coords(seq, grp):
    return 2 * (seq // 8) + grp // 8, (seq // 2) % 4, seq % 2, grp % 8


def device(x, y, core, z):
    return (8 * (x // 2) + 2 * y + core) * 16 + 8 * (x % 2) + z


def move(array, target):
    pairs = []
    for seq in range(16):
        for grp in range(16):
            pairs.append((16 * seq + grp, device(*target(*coords(seq, grp)))))
    return lax.ppermute(array, MESH, pairs)


def along_x(array, step):
    return move(array, lambda x, y, c, z: ((x + step) % 4, y, c, z))


def along_y(array, step):
    return move(array, lambda x, y, c, z: (x, (y + step) % 4, c, z))


def along_z(array, step):
    return move(array, lambda x, y, c, z: (x, y, c, (z + step) % 8))


def other_core(array):
    return move(array, lambda x, y, c, z: (x, y, 1 - c, z))


def other_x_lo(array):
    return move(array, lambda x, y, c, z: (x ^ 1, y, c, z))


def to_rows(array, first):
    def target(x, y, c, z):
        h, p = x // 2, x % 2
        return 2 * p + (h if first else 1 - h), z // 2, c, 2 * ((y - z // 2) % 4) + (z + h) % 2

    return move(array, target)


def after_kernel(n_after, *refs):
    sources, targets = refs[: len(refs) - n_after], refs[len(refs) - n_after :]
    n = 0
    for target in targets:
        for place in range(target.shape[0]):
            target[place] = sources[n][...]
            n += 1


def after(stacks, *earlier):
    pieces = [piece for stack in stacks for piece in stack]
    shapes = [jax.ShapeDtypeStruct((len(stack), *stack[0].shape), BF) for stack in stacks]
    return pl.pallas_call(
        lambda *refs: after_kernel(
            len(stacks), *refs[: len(pieces)], *refs[len(pieces) + len(earlier) :]
        ),
        in_specs=[VMEM] * (len(pieces) + len(earlier)),
        out_specs=[VMEM] * len(stacks),
        out_shape=shapes,
        compiler_params=pltpu.CompilerParams(vmem_limit_bytes=8 * MIB),
        cost_estimate=pl.CostEstimate(flops=0, bytes_accessed=10**6, transcendentals=0),
        name="after",
    )(*pieces, *earlier)


def angles(rows, cols, modulus):
    turned = (np.arange(rows)[:, None] * np.arange(cols)[None, :]) % modulus
    angle = turned.astype(np.float32) * np.float32(2.0 * math.pi / modulus)
    return np.cos(angle), np.sin(angle)


def tables():
    c_one, s_one = angles(128, 64, 128)
    order = np.array([4 * s + q for q in range(4) for s in range(16)])
    c_one, s_one = c_one[:, order], s_one[:, order]
    t_cos, t_sin = angles(128, 128, 16384)
    c_blk, s_blk = angles(128, 128, 128)
    first = np.concatenate([c_one, s_one], 0)
    last = np.concatenate([c_one.T, -s_one.T], 1) / 16384.0
    fwd = np.block([[c_blk, -s_blk], [s_blk, c_blk]])
    bwd = np.block([[c_blk, s_blk], [-s_blk, c_blk]])
    as_bf = [jnp.asarray(t, dtype=F32).astype(BF) for t in (first, last, fwd, bwd)]
    return (*as_bf, jnp.asarray(t_cos, dtype=F32), jnp.asarray(t_sin, dtype=F32))


def prepare_kernel(gate, key, value, filt, out):
    row = lax.broadcasted_iota(jnp.int32, (128, 128), 0)
    col = lax.broadcasted_iota(jnp.int32, (128, 128), 1)
    eye = (row == col).astype(BF)
    mixed = (key[...].astype(F32) * value[...].astype(F32)).astype(BF)
    for place, block in enumerate((mixed, filt[...], gate[...])):
        turned = lax.dot_general(
            eye, block, (((1,), (1,)), ((), ())), preferred_element_type=F32
        ).astype(BF)
        for j in range(4):
            out[j, 32 * place : 32 * place + 32, :] = turned[32 * j : 32 * j + 32, :]


def prepare(gate, key, value, filt):
    block = pl.BlockSpec((512, 128), lambda i: (0, i))
    return pl.pallas_call(
        prepare_kernel,
        grid=(4,),
        in_specs=[block] * 4,
        out_specs=pl.BlockSpec((4, 96, 512), lambda i: (i, 0, 0)),
        out_shape=jax.ShapeDtypeStruct((16, 96, 512), BF),
        name="prepare",
    )(gate, key, value, filt)


GROUP = 8


def conv_kernel(
    where, skip, data, first, last, fwd, bwd, t_cos, t_sin, keep_same, keep_other, send, grid, done
):
    for arr in range(3):
        for half in range(2):
            lo = 32 * arr + 16 * half
            block = data[:, lo : lo + 16, :].astype(F32)
            block = jnp.swapaxes(block, 0, 1).astype(BF)
            for i in range(16):
                for q in range(4):
                    grid[16 * q : 16 * q + 16, (lo + i) * 128 : (lo + i + 1) * 128] = block[
                        i, :, 128 * q : 128 * q + 128
                    ]
    tc = t_cos[...]
    ts = t_sin[...]

    def group(g, carry):
        lanes = pl.ds(pl.multiple_of(g * (GROUP * 128), GROUP * 128), GROUP * 128)
        f_lanes = pl.ds(pl.multiple_of(4096 + g * (GROUP * 128), GROUP * 128), GROUP * 128)
        g_lanes = pl.ds(pl.multiple_of(8192 + g * (GROUP * 128), GROUP * 128), GROUP * 128)
        spectra = []
        for where_lanes in (lanes, f_lanes):
            s = jnp.dot(first[...], grid[:, where_lanes], preferred_element_type=F32)
            rows = []
            for i in range(GROUP):
                s_re = s[:128, 128 * i : 128 * i + 128]
                s_im = -s[128:, 128 * i : 128 * i + 128]
                t_re = (s_re * tc + s_im * ts).astype(BF)
                t_im = (s_im * tc - s_re * ts).astype(BF)
                rows.append(jnp.concatenate([t_re, t_im], 1))
            spectra.append(
                jnp.dot(jnp.concatenate(rows, 0), fwd[...], preferred_element_type=F32)
            )
        u, f = spectra
        u_re, u_im, f_re, f_im = u[:, :128], u[:, 128:], f[:, :128], f[:, 128:]
        p_re = (u_re * f_re - u_im * f_im).astype(BF)
        p_im = (u_re * f_im + u_im * f_re).astype(BF)
        qq = jnp.dot(
            jnp.concatenate([p_re, p_im], 1), bwd[...], preferred_element_type=F32
        )
        cols = []
        for i in range(GROUP):
            q_re = qq[128 * i : 128 * i + 128, :128]
            q_im = qq[128 * i : 128 * i + 128, 128:]
            r_re = (q_re * tc - q_im * ts).astype(BF)
            r_im = (q_im * tc + q_re * ts).astype(BF)
            cols.append(jnp.concatenate([r_re, r_im], 0))
        conv = jnp.dot(last[...], jnp.concatenate(cols, 1), preferred_element_type=F32)
        signal = grid[:, lanes].astype(F32)
        gates = grid[:, g_lanes].astype(F32)
        for i in range(GROUP):
            part = slice(128 * i, 128 * i + 128)
            mixed_out = conv[:, part] + skip[g * GROUP + i] * signal[:, part]
            gated = gates[:, part] * mixed_out.astype(BF).astype(F32)
            done[g * GROUP + i] = gated
        return carry

    lax.fori_loop(0, 32 // GROUP, group, 0)
    core = where[2]
    x_lo = where[0] % 2

    def quarter(lo, part):
        rows = pl.ds(pl.multiple_of(part * 16, 16), 16)
        return jnp.swapaxes(done[lo : lo + 16, rows, :], 0, 1).astype(BF)

    for lo in (0, 16):
        keep_same[:, lo : lo + 16, :] = quarter(lo, 2 * x_lo + core)
        keep_other[:, lo : lo + 16, :] = quarter(lo, 2 * (1 - x_lo) + core)
        send[0, :, lo : lo + 16, :] = quarter(lo, 2 * x_lo + 1 - core)
        send[1, :, lo : lo + 16, :] = quarter(lo, 2 * (1 - x_lo) + 1 - core)


def convolve(where, skips, data):
    piece = jax.ShapeDtypeStruct((16, 32, 128), BF)
    return pl.pallas_call(
        conv_kernel,
        in_specs=[SMEM, SMEM] + [VMEM] * 7,
        out_specs=[VMEM] * 3,
        out_shape=[piece, piece, jax.ShapeDtypeStruct((2, 16, 32, 128), BF)],
        scratch_shapes=[pltpu.VMEM((64, 96 * 128), BF), pltpu.VMEM((32, 64, 128), F32)],
        compiler_params=pltpu.CompilerParams(vmem_limit_bytes=14 * MIB),
        cost_estimate=pl.CostEstimate(
            flops=4 * 10**9, bytes_accessed=3 * 10**6, transcendentals=0
        ),
        name="convolve",
    )(where, skips, data, *tables())


def columns_kernel(where, own, below, above, far, right):
    y, core = where[1], where[2]
    for j in range(2):
        from_x = where[4 + j]
        for step, shard in ((0, own), (-1, below), (1, above), (2, far)):
            from_y = (y + step + 4) % 4
            base = 32 * (8 * (from_x // 2) + 2 * from_y)
            for rel in range(2):
                row = pl.ds(pl.multiple_of(base + 32 * ((core + rel) % 2), 32), 32)
                for a in range(16):
                    right[row, 128 * a : 128 * a + 128] = shard[j, rel, a]


def columns(where, *shards):
    return pl.pallas_call(
        columns_kernel,
        in_specs=[SMEM] + [VMEM] * len(shards),
        out_specs=VMEM,
        out_shape=jax.ShapeDtypeStruct((512, 2048), BF),
        compiler_params=pltpu.CompilerParams(vmem_limit_bytes=12 * MIB),
        cost_estimate=pl.CostEstimate(flops=0, bytes_accessed=4 * 10**6, transcendentals=0),
        name="columns",
    )(where, *shards)


def gram_kernel(steps, n_right, n_earlier, where, *refs):
    rows = 64 * len(steps)
    rights, shard_refs = refs[:n_right], refs[n_right : -3 - n_earlier]
    keep, send, left = refs[-3:]
    x, core, z = where[0], where[2], where[3]
    shards = []
    for ref in shard_refs:
        shards += [(ref, j) for j in range(2)] if ref.shape[0] == 2 else [(ref, 0)]
    for n, (ref, j) in enumerate(shards):
        h = (x + n) % 2
        source = (z + steps[n // 2] + 8) % 8
        slot = (source + h + core) % 2
        for rel in range(2):
            row = rows * slot + 64 * (n // 2) + 32 * ((core + rel) % 2)
            row = pl.multiple_of(row, 32)
            for a in range(16):
                left[pl.ds(row, 32), 128 * a : 128 * a + 128] = ref[j, rel, a]
    for half, right in enumerate(rights):
        times(left, right, keep.at[half], send.at[half])


def times(left, right, keep, send):
    rows = keep.shape[0]
    for sub in range(2):
        lanes = slice(256 * sub, 256 * sub + 256)
        part = lax.dot_general(
            left[...],
            right[lanes, :],
            (((1,), (1,)), ((), ())),
            preferred_element_type=F32,
        )
        keep[:, lanes] = part[:rows]
        send[:, lanes] = part[rows:]


def again_kernel(left, right, keep, send):
    times(left, right, keep.at[0], send.at[0])


def gram_again(left, right):
    tile = jax.ShapeDtypeStruct((1, left.shape[0] // 2, 512), F32)
    return pl.pallas_call(
        again_kernel,
        in_specs=[VMEM] * 2,
        out_specs=[VMEM] * 2,
        out_shape=[tile, tile],
        compiler_params=pltpu.CompilerParams(vmem_limit_bytes=18 * MIB),
        cost_estimate=pl.CostEstimate(
            flops=2 * left.shape[0] * 512 * 2048, bytes_accessed=4 * 10**6, transcendentals=0
        ),
        name="gram_again",
    )(left, right)


def gram_part(steps, where, rights, shards, *earlier):
    rows = 64 * len(steps)
    tile = jax.ShapeDtypeStruct((len(rights), rows, 512), F32)
    return pl.pallas_call(
        functools.partial(gram_kernel, steps, len(rights), len(earlier)),
        in_specs=[SMEM] + [VMEM] * (len(rights) + len(shards) + len(earlier)),
        out_specs=[VMEM] * 3,
        out_shape=[tile, tile, jax.ShapeDtypeStruct((2 * rows, 2048), BF)],
        compiler_params=pltpu.CompilerParams(vmem_limit_bytes=18 * MIB),
        cost_estimate=pl.CostEstimate(
            flops=4 * rows * len(rights) * 512 * 2048,
            bytes_accessed=4 * 10**6,
            transcendentals=0,
        ),
        name="gram_part",
    )(where, *rights, *shards, *earlier)


def finish_kernel(chunks, where, running, *refs):
    out = refs[-1]
    y, core, z = where[1], where[2], where[3]
    for n, steps in enumerate(chunks):
        keep, got, theirs = refs[3 * n : 3 * n + 3]
        for k, step in enumerate(steps):
            source = (z + step + 8) % 8
            h = (source + core) % 2
            from_y = (y + source // 2) % 4
            rows = pl.ds(pl.multiple_of(64 * (4 * h + from_y), 64), 64)
            here = slice(64 * k, 64 * k + 64)
            total = keep[0, here, :] + got[0, here, :] + theirs[here, :]
            out[rows, :] = running[rows, :] + total * (1.0 / 8192.0)


def finish(chunks, where, running, *parts):
    specs = [SMEM, VMEM]
    for steps in chunks:
        half = pl.BlockSpec((1, 64 * len(steps), 512), lambda i: (0, 0, 0))
        specs += [half, half, pl.BlockSpec((64 * len(steps), 512), lambda i: (0, 0))]
    return pl.pallas_call(
        functools.partial(finish_kernel, chunks),
        grid=(1,),
        in_specs=specs,
        out_specs=VMEM,
        out_shape=jax.ShapeDtypeStruct((512, 512), F32),
        compiler_params=pltpu.CompilerParams(vmem_limit_bytes=12 * MIB),
        cost_estimate=pl.CostEstimate(flops=10**6, bytes_accessed=5 * 10**6, transcendentals=0),
        name="finish",
    )(where, running, *parts)


STEPS = (0, -1, 1, -2, 2, -3, 3, 4)
CHUNKS = (STEPS[:7], STEPS[7:])


def local(gate_in, key_in, value_in, filt_in, skip_gain, running_gram):
    seq, grp = lax.axis_index("seq"), lax.axis_index("grp")
    x, y, core, z = coords(seq, grp)
    where = jnp.stack([x, y, core, z, x, x]).astype(jnp.int32)
    across = jnp.stack([x, y, core, z, x, (x + 2) % 4]).astype(jnp.int32)
    beside = jnp.stack([x, y, core, z, (x + 1) % 4, (x + 3) % 4]).astype(jnp.int32)
    skips = lax.dynamic_slice_in_dim(skip_gain, seq * 32, 32, 0)

    outgoing = prepare(gate_in, key_in, value_in, filt_in)
    data = lax.all_to_all(outgoing, "seq", split_axis=0, concat_axis=0, tiled=True)
    same, other, send = convolve(where, skips, data)

    got = other_core(send)
    same = jnp.stack([same, got[0]])
    other = jnp.stack([other, got[1]])
    crossed = (x % 2) != (x // 2)
    row_a = to_rows(jnp.where(crossed, other, same), True)
    row_b = to_rows(jnp.where(crossed, same, other), False)
    below = along_x(other, 1)
    above = along_x(other, 3)
    opposite = along_x(same, 2)

    rows, near = after([[row_a, row_b], [above, below]], same, opposite)
    ups, downs = [rows], [rows]
    for _ in range(3):
        ups.append(along_z(ups[-1], 1))
        downs.append(along_z(downs[-1], 7))
    far = along_z(ups[3][:1], 1), along_z(downs[3][1:], 7)

    near_up, near_down = along_y(near, 1), along_y(near, 3)
    (own,) = after([[same, opposite]], near_up, near_down)
    near_far, own_down = along_y(near_up, 1), along_y(own, 3)
    own_up, own_far = along_y(own, 1), along_y(own_down, 3)
    right = columns(beside, near, near_up, near_down, near_far)
    own_right = columns(across, own, own_up, own_down, own_far)

    early = [rows, ups[1], downs[1], ups[2], downs[2], ups[3], downs[3]]
    keep, send, left = gram_part(CHUNKS[0], where, [right], early, own_right)
    theirs_a = other_x_lo(keep[0] + other_core(send)[0])
    keep_a, send_a = gram_again(left, own_right)
    got_a = other_core(send_a)

    keep_b, send_b, _ = gram_part(CHUNKS[1], where, [own_right, right], far)
    got_b = other_core(send_b)
    theirs_b = other_x_lo(keep_b[1] + got_b[1])
    return finish(
        CHUNKS, where, running_gram, keep_a, got_a, theirs_a, keep_b, got_b, theirs_b
    )


def solution(mesh):
    in_specs = (
        P("seq", "grp"),
        P("seq", "grp"),
        P("seq", "grp"),
        P("seq", "grp"),
        P("grp"),
        P("seq", "grp"),
    )
    out_specs = P("seq", "grp")
    return jax.shard_map(local, mesh=mesh, in_specs=in_specs, out_specs=out_specs, check_vma=False)
```

```python
import functools
import math

import jax
import jax.numpy as jnp
import numpy as np
from jax import lax
from jax.experimental import pallas as pl
from jax.experimental.pallas import tpu as pltpu
from jax.sharding import PartitionSpec as P

BF = jnp.bfloat16
F32 = jnp.float32
MESH = ("seq", "grp")
VMEM = pl.BlockSpec(memory_space=pltpu.VMEM)
SMEM = pl.BlockSpec(memory_space=pltpu.SMEM)
MIB = 1024 * 1024


def coords(seq, grp):
    return 2 * (seq // 8) + grp // 8, (seq // 2) % 4, seq % 2, grp % 8


def device(x, y, core, z):
    return (8 * (x // 2) + 2 * y + core) * 16 + 8 * (x % 2) + z


def move(array, target):
    pairs = []
    for seq in range(16):
        for grp in range(16):
            pairs.append((16 * seq + grp, device(*target(*coords(seq, grp)))))
    return lax.ppermute(array, MESH, pairs)


def along_x(array, step):
    return move(array, lambda x, y, c, z: ((x + step) % 4, y, c, z))


def along_y(array, step):
    return move(array, lambda x, y, c, z: (x, (y + step) % 4, c, z))


def along_z(array, step):
    return move(array, lambda x, y, c, z: (x, y, c, (z + step) % 8))


def other_core(array):
    return move(array, lambda x, y, c, z: (x, y, 1 - c, z))


def other_x_lo(array):
    return move(array, lambda x, y, c, z: (x ^ 1, y, c, z))


def to_rows(array, first):
    def target(x, y, c, z):
        h, p = x // 2, x % 2
        return 2 * p + (h if first else 1 - h), z // 2, c, 2 * ((y - z // 2) % 4) + (z + h) % 2

    return move(array, target)


def after_kernel(n_after, *refs):
    sources, targets = refs[: len(refs) - n_after], refs[len(refs) - n_after :]
    n = 0
    for target in targets:
        for place in range(target.shape[0]):
            target[place] = sources[n][...]
            n += 1


def after(stacks, *earlier):
    pieces = [piece for stack in stacks for piece in stack]
    shapes = [jax.ShapeDtypeStruct((len(stack), *stack[0].shape), BF) for stack in stacks]
    return pl.pallas_call(
        lambda *refs: after_kernel(
            len(stacks), *refs[: len(pieces)], *refs[len(pieces) + len(earlier) :]
        ),
        in_specs=[VMEM] * (len(pieces) + len(earlier)),
        out_specs=[VMEM] * len(stacks),
        out_shape=shapes,
        compiler_params=pltpu.CompilerParams(vmem_limit_bytes=8 * MIB),
        cost_estimate=pl.CostEstimate(flops=0, bytes_accessed=10**6, transcendentals=0),
        name="after",
    )(*pieces, *earlier)


def angles(rows, cols, modulus):
    turned = (np.arange(rows)[:, None] * np.arange(cols)[None, :]) % modulus
    angle = turned.astype(np.float32) * np.float32(2.0 * math.pi / modulus)
    return np.cos(angle), np.sin(angle)


def tables():
    c_one, s_one = angles(128, 64, 128)
    order = np.array([4 * s + q for q in range(4) for s in range(16)])
    c_one, s_one = c_one[:, order], s_one[:, order]
    t_cos, t_sin = angles(128, 128, 16384)
    c_blk, s_blk = angles(128, 128, 128)
    first = np.concatenate([c_one, s_one], 0)
    last = np.concatenate([c_one.T, -s_one.T], 1) / 16384.0
    fwd = np.block([[c_blk, -s_blk], [s_blk, c_blk]])
    bwd = np.block([[c_blk, s_blk], [-s_blk, c_blk]])
    as_bf = [jnp.asarray(t, dtype=F32).astype(BF) for t in (first, last, fwd, bwd)]
    return (*as_bf, jnp.asarray(t_cos, dtype=F32), jnp.asarray(t_sin, dtype=F32))


def prepare_kernel(gate, key, value, filt, out):
    row = lax.broadcasted_iota(jnp.int32, (128, 128), 0)
    col = lax.broadcasted_iota(jnp.int32, (128, 128), 1)
    eye = (row == col).astype(BF)
    mixed = (key[...].astype(F32) * value[...].astype(F32)).astype(BF)
    for place, block in enumerate((mixed, filt[...], gate[...])):
        for part in range(4):
            turned = lax.dot_general(
                eye,
                block[:, 128 * part : 128 * part + 128],
                (((1,), (1,)), ((), ())),
                preferred_element_type=F32,
            ).astype(BF)
            for j in range(4):
                out[4 * part + j, 32 * place : 32 * place + 32, :] = turned[
                    32 * j : 32 * j + 32, :
                ]


def prepare(gate, key, value, filt):
    return pl.pallas_call(
        prepare_kernel,
        in_specs=[VMEM] * 4,
        out_specs=VMEM,
        out_shape=jax.ShapeDtypeStruct((16, 96, 512), BF),
        compiler_params=pltpu.CompilerParams(vmem_limit_bytes=16 * MIB),
        cost_estimate=pl.CostEstimate(
            flops=10**8, bytes_accessed=4 * 10**6, transcendentals=0
        ),
        name="prepare",
    )(gate, key, value, filt)


GROUP = 8


def conv_kernel(
    where, skip, data, first, last, fwd, bwd, t_cos, t_sin, keep_same, keep_other, send, grid, done
):
    for arr in range(3):
        for half in range(2):
            lo = 32 * arr + 16 * half
            block = data[:, lo : lo + 16, :].astype(F32)
            block = jnp.swapaxes(block, 0, 1).astype(BF)
            for i in range(16):
                for q in range(4):
                    grid[16 * q : 16 * q + 16, (lo + i) * 128 : (lo + i + 1) * 128] = block[
                        i, :, 128 * q : 128 * q + 128
                    ]
    tc = t_cos[...]
    ts = t_sin[...]

    def group(g, carry):
        lanes = pl.ds(pl.multiple_of(g * (GROUP * 128), GROUP * 128), GROUP * 128)
        f_lanes = pl.ds(pl.multiple_of(4096 + g * (GROUP * 128), GROUP * 128), GROUP * 128)
        g_lanes = pl.ds(pl.multiple_of(8192 + g * (GROUP * 128), GROUP * 128), GROUP * 128)
        spectra = []
        for where_lanes in (lanes, f_lanes):
            s = jnp.dot(first[...], grid[:, where_lanes], preferred_element_type=F32)
            rows = []
            for i in range(GROUP):
                s_re = s[:128, 128 * i : 128 * i + 128]
                s_im = -s[128:, 128 * i : 128 * i + 128]
                t_re = (s_re * tc + s_im * ts).astype(BF)
                t_im = (s_im * tc - s_re * ts).astype(BF)
                rows.append(jnp.concatenate([t_re, t_im], 1))
            spectra.append(
                jnp.dot(jnp.concatenate(rows, 0), fwd[...], preferred_element_type=F32)
            )
        u, f = spectra
        u_re, u_im, f_re, f_im = u[:, :128], u[:, 128:], f[:, :128], f[:, 128:]
        p_re = (u_re * f_re - u_im * f_im).astype(BF)
        p_im = (u_re * f_im + u_im * f_re).astype(BF)
        qq = jnp.dot(
            jnp.concatenate([p_re, p_im], 1), bwd[...], preferred_element_type=F32
        )
        cols = []
        for i in range(GROUP):
            q_re = qq[128 * i : 128 * i + 128, :128]
            q_im = qq[128 * i : 128 * i + 128, 128:]
            r_re = (q_re * tc - q_im * ts).astype(BF)
            r_im = (q_im * tc + q_re * ts).astype(BF)
            cols.append(jnp.concatenate([r_re, r_im], 0))
        conv = jnp.dot(last[...], jnp.concatenate(cols, 1), preferred_element_type=F32)
        signal = grid[:, lanes].astype(F32)
        gates = grid[:, g_lanes].astype(F32)
        for i in range(GROUP):
            part = slice(128 * i, 128 * i + 128)
            mixed_out = conv[:, part] + skip[g * GROUP + i] * signal[:, part]
            gated = gates[:, part] * mixed_out.astype(BF).astype(F32)
            done[g * GROUP + i] = gated
        return carry

    lax.fori_loop(0, 32 // GROUP, group, 0)
    core = where[2]
    x_lo = where[0] % 2

    def quarter(lo, part):
        rows = pl.ds(pl.multiple_of(part * 16, 16), 16)
        return jnp.swapaxes(done[lo : lo + 16, rows, :], 0, 1).astype(BF)

    for lo in (0, 16):
        keep_same[:, lo : lo + 16, :] = quarter(lo, 2 * x_lo + core)
        keep_other[:, lo : lo + 16, :] = quarter(lo, 2 * (1 - x_lo) + core)
        send[0, :, lo : lo + 16, :] = quarter(lo, 2 * x_lo + 1 - core)
        send[1, :, lo : lo + 16, :] = quarter(lo, 2 * (1 - x_lo) + 1 - core)


def convolve(where, skips, data):
    piece = jax.ShapeDtypeStruct((16, 32, 128), BF)
    return pl.pallas_call(
        conv_kernel,
        in_specs=[SMEM, SMEM] + [VMEM] * 7,
        out_specs=[VMEM] * 3,
        out_shape=[piece, piece, jax.ShapeDtypeStruct((2, 16, 32, 128), BF)],
        scratch_shapes=[pltpu.VMEM((64, 96 * 128), BF), pltpu.VMEM((32, 64, 128), F32)],
        compiler_params=pltpu.CompilerParams(vmem_limit_bytes=14 * MIB),
        cost_estimate=pl.CostEstimate(
            flops=4 * 10**9, bytes_accessed=3 * 10**6, transcendentals=0
        ),
        name="convolve",
    )(where, skips, data, *tables())


def columns_kernel(where, own, below, above, far_low, far_high, right):
    y, core = where[1], where[2]
    for j in range(2):
        from_x = where[4 + j]
        for step in (0, -1, 1, 2):
            from_y = (y + step + 4) % 4
            base = 32 * (8 * (from_x // 2) + 2 * from_y)
            for rel in range(2):
                row = pl.ds(pl.multiple_of(base + 32 * ((core + rel) % 2), 32), 32)
                if step == 2:
                    piece = (far_low, far_high)[rel].at[j, 0]
                else:
                    piece = {0: own, -1: below, 1: above}[step].at[j, rel]
                for a in range(16):
                    right[row, 128 * a : 128 * a + 128] = piece[a]


def columns(where, *shards):
    return pl.pallas_call(
        columns_kernel,
        in_specs=[SMEM] + [VMEM] * len(shards),
        out_specs=VMEM,
        out_shape=jax.ShapeDtypeStruct((512, 2048), BF),
        compiler_params=pltpu.CompilerParams(vmem_limit_bytes=12 * MIB),
        cost_estimate=pl.CostEstimate(flops=0, bytes_accessed=4 * 10**6, transcendentals=0),
        name="columns",
    )(where, *shards)


def gram_kernel(steps, n_right, n_earlier, where, *refs):
    rows = 64 * len(steps)
    rights, shard_refs = refs[:n_right], refs[n_right : -3 - n_earlier]
    keep, send, left = refs[-3:]
    x, core, z = where[0], where[2], where[3]
    shards = []
    for ref in shard_refs:
        shards += [(ref, j) for j in range(2)] if ref.shape[0] == 2 else [(ref, 0)]
    for n, (ref, j) in enumerate(shards):
        h = (x + n) % 2
        source = (z + steps[n // 2] + 8) % 8
        slot = (source + h + core) % 2
        for rel in range(2):
            row = rows * slot + 64 * (n // 2) + 32 * ((core + rel) % 2)
            row = pl.multiple_of(row, 32)
            for a in range(16):
                left[pl.ds(row, 32), 128 * a : 128 * a + 128] = ref[j, rel, a]
    for half, right in enumerate(rights):
        times(left, right, keep.at[half], send.at[half])


def times(left, right, keep, send):
    rows = keep.shape[0]
    for sub in range(2):
        lanes = slice(256 * sub, 256 * sub + 256)
        part = lax.dot_general(
            left[...],
            right[lanes, :],
            (((1,), (1,)), ((), ())),
            preferred_element_type=F32,
        )
        keep[:, lanes] = part[:rows]
        send[:, lanes] = part[rows:]


def again_kernel(left, right, keep, send):
    times(left, right, keep.at[0], send.at[0])


def gram_again(left, right):
    tile = jax.ShapeDtypeStruct((1, left.shape[0] // 2, 512), F32)
    return pl.pallas_call(
        again_kernel,
        in_specs=[VMEM] * 2,
        out_specs=[VMEM] * 2,
        out_shape=[tile, tile],
        compiler_params=pltpu.CompilerParams(vmem_limit_bytes=18 * MIB),
        cost_estimate=pl.CostEstimate(
            flops=2 * left.shape[0] * 512 * 2048, bytes_accessed=4 * 10**6, transcendentals=0
        ),
        name="gram_again",
    )(left, right)


def gram_part(steps, where, rights, shards, *earlier):
    rows = 64 * len(steps)
    tile = jax.ShapeDtypeStruct((len(rights), rows, 512), F32)
    return pl.pallas_call(
        functools.partial(gram_kernel, steps, len(rights), len(earlier)),
        in_specs=[SMEM] + [VMEM] * (len(rights) + len(shards) + len(earlier)),
        out_specs=[VMEM] * 3,
        out_shape=[tile, tile, jax.ShapeDtypeStruct((2 * rows, 2048), BF)],
        compiler_params=pltpu.CompilerParams(vmem_limit_bytes=18 * MIB),
        cost_estimate=pl.CostEstimate(
            flops=4 * rows * len(rights) * 512 * 2048,
            bytes_accessed=4 * 10**6,
            transcendentals=0,
        ),
        name="gram_part",
    )(where, *rights, *shards, *earlier)


def finish_kernel(chunks, where, running, *refs):
    out = refs[-1]
    y, core, z = where[1], where[2], where[3]
    for n, steps in enumerate(chunks):
        keep, got, theirs = refs[3 * n : 3 * n + 3]
        for k, step in enumerate(steps):
            source = (z + step + 8) % 8
            h = (source + core) % 2
            from_y = (y + source // 2) % 4
            rows = pl.ds(pl.multiple_of(64 * (4 * h + from_y), 64), 64)
            here = slice(64 * k, 64 * k + 64)
            total = keep[0, here, :] + got[0, here, :] + theirs[here, :]
            out[rows, :] = running[rows, :] + total * (1.0 / 8192.0)


def finish(chunks, where, running, *parts):
    specs = [SMEM, VMEM]
    for steps in chunks:
        half = pl.BlockSpec((1, 64 * len(steps), 512), lambda i: (0, 0, 0))
        specs += [half, half, pl.BlockSpec((64 * len(steps), 512), lambda i: (0, 0))]
    return pl.pallas_call(
        functools.partial(finish_kernel, chunks),
        grid=(1,),
        in_specs=specs,
        out_specs=VMEM,
        out_shape=jax.ShapeDtypeStruct((512, 512), F32),
        compiler_params=pltpu.CompilerParams(vmem_limit_bytes=12 * MIB),
        cost_estimate=pl.CostEstimate(flops=10**6, bytes_accessed=5 * 10**6, transcendentals=0),
        name="finish",
    )(where, running, *parts)


STEPS = (0, -1, 1, -2, 2, -3, 3, 4)
CHUNKS = (STEPS[:7], STEPS[7:])


def local(gate_in, key_in, value_in, filt_in, skip_gain, running_gram):
    seq, grp = lax.axis_index("seq"), lax.axis_index("grp")
    x, y, core, z = coords(seq, grp)
    where = jnp.stack([x, y, core, z, x, x]).astype(jnp.int32)
    across = jnp.stack([x, y, core, z, x, (x + 2) % 4]).astype(jnp.int32)
    beside = jnp.stack([x, y, core, z, (x + 1) % 4, (x + 3) % 4]).astype(jnp.int32)
    skips = lax.dynamic_slice_in_dim(skip_gain, seq * 32, 32, 0)

    outgoing = prepare(gate_in, key_in, value_in, filt_in)
    data = lax.all_to_all(outgoing, "seq", split_axis=0, concat_axis=0, tiled=True)
    same, other, send = convolve(where, skips, data)

    got = other_core(send)
    same = jnp.stack([same, got[0]])
    other = jnp.stack([other, got[1]])
    crossed = (x % 2) != (x // 2)
    row_a = to_rows(jnp.where(crossed, other, same), True)
    row_b = to_rows(jnp.where(crossed, same, other), False)
    below = along_x(other, 1)
    above = along_x(other, 3)
    opposite = along_x(same, 2)

    rows, near = after([[row_a, row_b], [above, below]], same, opposite)
    ups, downs = [rows], [rows]
    for _ in range(3):
        ups.append(along_z(ups[-1], 1))
        downs.append(along_z(downs[-1], 7))
    far = along_z(ups[3][:1], 1), along_z(downs[3][1:], 7)

    near_up, near_down = along_y(near, 1), along_y(near, 3)
    (own,) = after([[same, opposite]], near_up, near_down)
    near_far = along_y(near_up[:, :1], 1), along_y(near_down[:, 1:], 3)
    own_up, own_down = along_y(own, 1), along_y(own, 3)
    own_far = along_y(own_up[:, :1], 1), along_y(own_down[:, 1:], 3)
    right = columns(beside, near, near_up, near_down, *near_far)
    own_right = columns(across, own, own_up, own_down, *own_far)

    early = [rows, ups[1], downs[1], ups[2], downs[2], ups[3], downs[3]]
    keep, send, left = gram_part(CHUNKS[0], where, [right], early, own_right)
    theirs_a = other_x_lo(keep[0] + other_core(send)[0])
    keep_a, send_a = gram_again(left, own_right)
    got_a = other_core(send_a)

    keep_b, send_b, _ = gram_part(CHUNKS[1], where, [own_right, right], far)
    got_b = other_core(send_b)
    theirs_b = other_x_lo(keep_b[1] + got_b[1])
    return finish(
        CHUNKS, where, running_gram, keep_a, got_a, theirs_a, keep_b, got_b, theirs_b
    )


def solution(mesh):
    in_specs = (
        P("seq", "grp"),
        P("seq", "grp"),
        P("seq", "grp"),
        P("seq", "grp"),
        P("grp"),
        P("seq", "grp"),
    )
    out_specs = P("seq", "grp")
    return jax.shard_map(local, mesh=mesh, in_specs=in_specs, out_specs=out_specs, check_vma=False)
```

```python
import functools
import math

import jax
import jax.numpy as jnp
import numpy as np
from jax import lax
from jax.experimental import pallas as pl
from jax.experimental.pallas import tpu as pltpu
from jax.sharding import PartitionSpec as P

BF = jnp.bfloat16
F32 = jnp.float32
MESH = ("seq", "grp")
VMEM = pl.BlockSpec(memory_space=pltpu.VMEM)
SMEM = pl.BlockSpec(memory_space=pltpu.SMEM)
MIB = 1024 * 1024


def coords(seq, grp):
    return 2 * (seq // 8) + grp // 8, (seq // 2) % 4, seq % 2, grp % 8


def device(x, y, core, z):
    return (8 * (x // 2) + 2 * y + core) * 16 + 8 * (x % 2) + z


def move(array, target):
    pairs = []
    for seq in range(16):
        for grp in range(16):
            pairs.append((16 * seq + grp, device(*target(*coords(seq, grp)))))
    return lax.ppermute(array, MESH, pairs)


def along_x(array, step):
    return move(array, lambda x, y, c, z: ((x + step) % 4, y, c, z))


def along_y(array, step):
    return move(array, lambda x, y, c, z: (x, (y + step) % 4, c, z))


def along_z(array, step):
    return move(array, lambda x, y, c, z: (x, y, c, (z + step) % 8))


def other_core(array):
    return move(array, lambda x, y, c, z: (x, y, 1 - c, z))


def other_x_lo(array):
    return move(array, lambda x, y, c, z: (x ^ 1, y, c, z))


def to_rows(array, first):
    def target(x, y, c, z):
        h, p = x // 2, x % 2
        return 2 * p + (h if first else 1 - h), z // 2, c, 2 * ((y - z // 2) % 4) + (z + h) % 2

    return move(array, target)


def after_kernel(n_after, *refs):
    sources, targets = refs[: len(refs) - n_after], refs[len(refs) - n_after :]
    n = 0
    for target in targets:
        for place in range(target.shape[0]):
            target[place] = sources[n][...]
            n += 1


def after(stacks, *earlier):
    pieces = [piece for stack in stacks for piece in stack]
    shapes = [jax.ShapeDtypeStruct((len(stack), *stack[0].shape), BF) for stack in stacks]
    return pl.pallas_call(
        lambda *refs: after_kernel(
            len(stacks), *refs[: len(pieces)], *refs[len(pieces) + len(earlier) :]
        ),
        in_specs=[VMEM] * (len(pieces) + len(earlier)),
        out_specs=[VMEM] * len(stacks),
        out_shape=shapes,
        compiler_params=pltpu.CompilerParams(vmem_limit_bytes=8 * MIB),
        cost_estimate=pl.CostEstimate(flops=0, bytes_accessed=10**6, transcendentals=0),
        name="after",
    )(*pieces, *earlier)


def angles(rows, cols, modulus):
    turned = (np.arange(rows)[:, None] * np.arange(cols)[None, :]) % modulus
    angle = turned.astype(np.float32) * np.float32(2.0 * math.pi / modulus)
    return np.cos(angle), np.sin(angle)


def tables():
    c_one, s_one = angles(128, 64, 128)
    order = np.array([4 * s + q for q in range(4) for s in range(16)])
    c_one, s_one = c_one[:, order], s_one[:, order]
    t_cos, t_sin = angles(128, 128, 16384)
    c_blk, s_blk = angles(128, 128, 128)
    first = np.concatenate([c_one, s_one], 0)
    last = np.concatenate([c_one.T, -s_one.T], 1) / 16384.0
    fwd = np.block([[c_blk, -s_blk], [s_blk, c_blk]])
    bwd = np.block([[c_blk, s_blk], [-s_blk, c_blk]])
    as_bf = [jnp.asarray(t, dtype=F32).astype(BF) for t in (first, last, fwd, bwd)]
    return (*as_bf, jnp.asarray(t_cos, dtype=F32), jnp.asarray(t_sin, dtype=F32))


def prepare_kernel(gate, key, value, filt, out):
    row = lax.broadcasted_iota(jnp.int32, (128, 128), 0)
    col = lax.broadcasted_iota(jnp.int32, (128, 128), 1)
    eye = (row == col).astype(BF)
    mixed = (key[...].astype(F32) * value[...].astype(F32)).astype(BF)
    for place, block in enumerate((mixed, filt[...], gate[...])):
        turned = lax.dot_general(
            eye, block, (((1,), (1,)), ((), ())), preferred_element_type=F32
        ).astype(BF)
        for j in range(4):
            out[j, 32 * place : 32 * place + 32, :] = turned[32 * j : 32 * j + 32, :]


def prepare(gate, key, value, filt):
    block = pl.BlockSpec((512, 128), lambda i: (0, i))
    return pl.pallas_call(
        prepare_kernel,
        grid=(4,),
        in_specs=[block] * 4,
        out_specs=pl.BlockSpec((4, 96, 512), lambda i: (i, 0, 0)),
        out_shape=jax.ShapeDtypeStruct((16, 96, 512), BF),
        name="prepare",
    )(gate, key, value, filt)


GROUP = 8


def conv_kernel(
    where, skip, data, first, last, fwd, bwd, t_cos, t_sin, keep_same, keep_other, send, grid, done
):
    for arr in range(3):
        for half in range(2):
            lo = 32 * arr + 16 * half
            block = data[:, lo : lo + 16, :].astype(F32)
            block = jnp.swapaxes(block, 0, 1).astype(BF)
            for i in range(16):
                for q in range(4):
                    grid[16 * q : 16 * q + 16, (lo + i) * 128 : (lo + i + 1) * 128] = block[
                        i, :, 128 * q : 128 * q + 128
                    ]
    tc = t_cos[...]
    ts = t_sin[...]

    def group(g, carry):
        lanes = pl.ds(pl.multiple_of(g * (GROUP * 128), GROUP * 128), GROUP * 128)
        f_lanes = pl.ds(pl.multiple_of(4096 + g * (GROUP * 128), GROUP * 128), GROUP * 128)
        g_lanes = pl.ds(pl.multiple_of(8192 + g * (GROUP * 128), GROUP * 128), GROUP * 128)
        spectra = []
        for where_lanes in (lanes, f_lanes):
            s = jnp.dot(first[...], grid[:, where_lanes], preferred_element_type=F32)
            rows = []
            for i in range(GROUP):
                s_re = s[:128, 128 * i : 128 * i + 128]
                s_im = -s[128:, 128 * i : 128 * i + 128]
                t_re = (s_re * tc + s_im * ts).astype(BF)
                t_im = (s_im * tc - s_re * ts).astype(BF)
                rows.append(jnp.concatenate([t_re, t_im], 1))
            spectra.append(
                jnp.dot(jnp.concatenate(rows, 0), fwd[...], preferred_element_type=F32)
            )
        u, f = spectra
        u_re, u_im, f_re, f_im = u[:, :128], u[:, 128:], f[:, :128], f[:, 128:]
        p_re = (u_re * f_re - u_im * f_im).astype(BF)
        p_im = (u_re * f_im + u_im * f_re).astype(BF)
        qq = jnp.dot(
            jnp.concatenate([p_re, p_im], 1), bwd[...], preferred_element_type=F32
        )
        cols = []
        for i in range(GROUP):
            q_re = qq[128 * i : 128 * i + 128, :128]
            q_im = qq[128 * i : 128 * i + 128, 128:]
            r_re = (q_re * tc - q_im * ts).astype(BF)
            r_im = (q_im * tc + q_re * ts).astype(BF)
            cols.append(jnp.concatenate([r_re, r_im], 0))
        conv = jnp.dot(last[...], jnp.concatenate(cols, 1), preferred_element_type=F32)
        signal = grid[:, lanes].astype(F32)
        gates = grid[:, g_lanes].astype(F32)
        for i in range(GROUP):
            part = slice(128 * i, 128 * i + 128)
            mixed_out = conv[:, part] + skip[g * GROUP + i] * signal[:, part]
            gated = gates[:, part] * mixed_out.astype(BF).astype(F32)
            done[g * GROUP + i] = gated
        return carry

    lax.fori_loop(0, 32 // GROUP, group, 0)
    core = where[2]
    x_lo = where[0] % 2

    def quarter(lo, part):
        rows = pl.ds(pl.multiple_of(part * 16, 16), 16)
        return jnp.swapaxes(done[lo : lo + 16, rows, :], 0, 1).astype(BF)

    for lo in (0, 16):
        keep_same[:, lo : lo + 16, :] = quarter(lo, 2 * x_lo + core)
        keep_other[:, lo : lo + 16, :] = quarter(lo, 2 * (1 - x_lo) + core)
        send[0, :, lo : lo + 16, :] = quarter(lo, 2 * x_lo + 1 - core)
        send[1, :, lo : lo + 16, :] = quarter(lo, 2 * (1 - x_lo) + 1 - core)


def convolve(where, skips, data):
    piece = jax.ShapeDtypeStruct((16, 32, 128), BF)
    return pl.pallas_call(
        conv_kernel,
        in_specs=[SMEM, SMEM] + [VMEM] * 7,
        out_specs=[VMEM] * 3,
        out_shape=[piece, piece, jax.ShapeDtypeStruct((2, 16, 32, 128), BF)],
        scratch_shapes=[pltpu.VMEM((64, 96 * 128), BF), pltpu.VMEM((32, 64, 128), F32)],
        compiler_params=pltpu.CompilerParams(vmem_limit_bytes=14 * MIB),
        cost_estimate=pl.CostEstimate(
            flops=4 * 10**9, bytes_accessed=3 * 10**6, transcendentals=0
        ),
        name="convolve",
    )(where, skips, data, *tables())


def columns_kernel(where, own, below, above, far_low, far_high, right):
    y, core = where[1], where[2]
    for j in range(2):
        from_x = where[4 + j]
        for step in (0, -1, 1, 2):
            from_y = (y + step + 4) % 4
            base = 32 * (8 * (from_x // 2) + 2 * from_y)
            for rel in range(2):
                row = pl.ds(pl.multiple_of(base + 32 * ((core + rel) % 2), 32), 32)
                if step == 2:
                    piece = (far_low, far_high)[rel].at[j, 0]
                else:
                    piece = {0: own, -1: below, 1: above}[step].at[j, rel]
                for a in range(16):
                    right[row, 128 * a : 128 * a + 128] = piece[a]


def columns(where, *shards):
    return pl.pallas_call(
        columns_kernel,
        in_specs=[SMEM] + [VMEM] * len(shards),
        out_specs=VMEM,
        out_shape=jax.ShapeDtypeStruct((512, 2048), BF),
        compiler_params=pltpu.CompilerParams(vmem_limit_bytes=12 * MIB),
        cost_estimate=pl.CostEstimate(flops=0, bytes_accessed=4 * 10**6, transcendentals=0),
        name="columns",
    )(where, *shards)


def gram_kernel(steps, n_right, n_earlier, where, *refs):
    rows = 64 * len(steps)
    rights, shard_refs = refs[:n_right], refs[n_right : -3 - n_earlier]
    keep, send, left = refs[-3:]
    x, core, z = where[0], where[2], where[3]
    shards = []
    for ref in shard_refs:
        shards += [(ref, j) for j in range(2)] if ref.shape[0] == 2 else [(ref, 0)]
    for n, (ref, j) in enumerate(shards):
        h = (x + n) % 2
        source = (z + steps[n // 2] + 8) % 8
        slot = (source + h + core) % 2
        for rel in range(2):
            row = rows * slot + 64 * (n // 2) + 32 * ((core + rel) % 2)
            row = pl.multiple_of(row, 32)
            for a in range(16):
                left[pl.ds(row, 32), 128 * a : 128 * a + 128] = ref[j, rel, a]
    for half, right in enumerate(rights):
        times(left, right, keep.at[half], send.at[half])


def times(left, right, keep, send):
    rows = keep.shape[0]
    for sub in range(2):
        lanes = slice(256 * sub, 256 * sub + 256)
        part = lax.dot_general(
            left[...],
            right[lanes, :],
            (((1,), (1,)), ((), ())),
            preferred_element_type=F32,
        )
        keep[:, lanes] = part[:rows]
        send[:, lanes] = part[rows:]


def again_kernel(left, right, keep, send):
    times(left, right, keep.at[0], send.at[0])


def gram_again(left, right):
    tile = jax.ShapeDtypeStruct((1, left.shape[0] // 2, 512), F32)
    return pl.pallas_call(
        again_kernel,
        in_specs=[VMEM] * 2,
        out_specs=[VMEM] * 2,
        out_shape=[tile, tile],
        compiler_params=pltpu.CompilerParams(vmem_limit_bytes=18 * MIB),
        cost_estimate=pl.CostEstimate(
            flops=2 * left.shape[0] * 512 * 2048, bytes_accessed=4 * 10**6, transcendentals=0
        ),
        name="gram_again",
    )(left, right)


def gram_part(steps, where, rights, shards, *earlier):
    rows = 64 * len(steps)
    tile = jax.ShapeDtypeStruct((len(rights), rows, 512), F32)
    return pl.pallas_call(
        functools.partial(gram_kernel, steps, len(rights), len(earlier)),
        in_specs=[SMEM] + [VMEM] * (len(rights) + len(shards) + len(earlier)),
        out_specs=[VMEM] * 3,
        out_shape=[tile, tile, jax.ShapeDtypeStruct((2 * rows, 2048), BF)],
        compiler_params=pltpu.CompilerParams(vmem_limit_bytes=18 * MIB),
        cost_estimate=pl.CostEstimate(
            flops=4 * rows * len(rights) * 512 * 2048,
            bytes_accessed=4 * 10**6,
            transcendentals=0,
        ),
        name="gram_part",
    )(where, *rights, *shards, *earlier)


def finish_kernel(chunks, where, running, *refs):
    out = refs[-1]
    y, core, z = where[1], where[2], where[3]
    for n, steps in enumerate(chunks):
        keep, got, theirs = refs[3 * n : 3 * n + 3]
        for k, step in enumerate(steps):
            source = (z + step + 8) % 8
            h = (source + core) % 2
            from_y = (y + source // 2) % 4
            rows = pl.ds(pl.multiple_of(64 * (4 * h + from_y), 64), 64)
            here = slice(64 * k, 64 * k + 64)
            total = keep[0, here, :] + got[0, here, :] + theirs[here, :]
            out[rows, :] = running[rows, :] + total * (1.0 / 8192.0)


def finish(chunks, where, running, *parts):
    specs = [SMEM, VMEM]
    for steps in chunks:
        half = pl.BlockSpec((1, 64 * len(steps), 512), lambda i: (0, 0, 0))
        specs += [half, half, pl.BlockSpec((64 * len(steps), 512), lambda i: (0, 0))]
    return pl.pallas_call(
        functools.partial(finish_kernel, chunks),
        grid=(1,),
        in_specs=specs,
        out_specs=VMEM,
        out_shape=jax.ShapeDtypeStruct((512, 512), F32),
        compiler_params=pltpu.CompilerParams(vmem_limit_bytes=12 * MIB),
        cost_estimate=pl.CostEstimate(flops=10**6, bytes_accessed=5 * 10**6, transcendentals=0),
        name="finish",
    )(where, running, *parts)


STEPS = (0, -1, 1, -2, 2, -3, 3, 4)
CHUNKS = (STEPS[:7], STEPS[7:])


def local(gate_in, key_in, value_in, filt_in, skip_gain, running_gram):
    seq, grp = lax.axis_index("seq"), lax.axis_index("grp")
    x, y, core, z = coords(seq, grp)
    where = jnp.stack([x, y, core, z, x, x]).astype(jnp.int32)
    across = jnp.stack([x, y, core, z, x, (x + 2) % 4]).astype(jnp.int32)
    beside = jnp.stack([x, y, core, z, (x + 1) % 4, (x + 3) % 4]).astype(jnp.int32)
    skips = lax.dynamic_slice_in_dim(skip_gain, seq * 32, 32, 0)

    outgoing = prepare(gate_in, key_in, value_in, filt_in)
    data = lax.all_to_all(outgoing, "seq", split_axis=0, concat_axis=0, tiled=True)
    same, other, send = convolve(where, skips, data)

    got = other_core(send)
    same = jnp.stack([same, got[0]])
    other = jnp.stack([other, got[1]])
    crossed = (x % 2) != (x // 2)
    row_a = to_rows(jnp.where(crossed, other, same), True)
    row_b = to_rows(jnp.where(crossed, same, other), False)
    below = along_x(other, 1)
    above = along_x(other, 3)
    opposite = along_x(same, 2)

    rows, near = after([[row_a, row_b], [above, below]], same, opposite)
    ups, downs = [rows], [rows]
    for _ in range(3):
        ups.append(along_z(ups[-1], 1))
        downs.append(along_z(downs[-1], 7))
    far = along_z(ups[3][:1], 1), along_z(downs[3][1:], 7)

    near_up, near_down = along_y(near, 1), along_y(near, 3)
    (own,) = after([[same, opposite]], near_up, near_down)
    near_far = along_y(near_up[:, :1], 1), along_y(near_down[:, 1:], 3)
    own_up, own_down = along_y(own, 1), along_y(own, 3)
    own_far = along_y(own_up[:, :1], 1), along_y(own_down[:, 1:], 3)
    right = columns(beside, near, near_up, near_down, *near_far)
    own_right = columns(across, own, own_up, own_down, *own_far)

    early = [rows, ups[1], downs[1], ups[2], downs[2], ups[3], downs[3]]
    keep, send, left = gram_part(CHUNKS[0], where, [right], early, own_right)
    theirs_a = other_x_lo(keep[0] + other_core(send)[0])
    keep_a, send_a = gram_again(left, own_right)
    got_a = other_core(send_a)

    keep_b, send_b, _ = gram_part(CHUNKS[1], where, [own_right, right], far)
    got_b = other_core(send_b)
    theirs_b = other_x_lo(keep_b[1] + got_b[1])
    return finish(
        CHUNKS, where, running_gram, keep_a, got_a, theirs_a, keep_b, got_b, theirs_b
    )


def solution(mesh):
    in_specs = (
        P("seq", "grp"),
        P("seq", "grp"),
        P("seq", "grp"),
        P("seq", "grp"),
        P("grp"),
        P("seq", "grp"),
    )
    out_specs = P("seq", "grp")
    return jax.shard_map(local, mesh=mesh, in_specs=in_specs, out_specs=out_specs, check_vma=False)
```

```python
import functools
import math

import jax
import jax.numpy as jnp
import numpy as np
from jax import lax
from jax.experimental import pallas as pl
from jax.experimental.pallas import tpu as pltpu
from jax.sharding import PartitionSpec as P

BF = jnp.bfloat16
F32 = jnp.float32
MESH = ("seq", "grp")
VMEM = pl.BlockSpec(memory_space=pltpu.VMEM)
SMEM = pl.BlockSpec(memory_space=pltpu.SMEM)
MIB = 1024 * 1024


def coords(seq, grp):
    return 2 * (seq // 8) + grp // 8, (seq // 2) % 4, seq % 2, grp % 8


def device(x, y, core, z):
    return (8 * (x // 2) + 2 * y + core) * 16 + 8 * (x % 2) + z


def move(array, target):
    pairs = []
    for seq in range(16):
        for grp in range(16):
            pairs.append((16 * seq + grp, device(*target(*coords(seq, grp)))))
    return lax.ppermute(array, MESH, pairs)


def along_x(array, step):
    return move(array, lambda x, y, c, z: ((x + step) % 4, y, c, z))


def along_y(array, step):
    return move(array, lambda x, y, c, z: (x, (y + step) % 4, c, z))


def along_z(array, step):
    return move(array, lambda x, y, c, z: (x, y, c, (z + step) % 8))


def other_core(array):
    return move(array, lambda x, y, c, z: (x, y, 1 - c, z))


def other_x_lo(array):
    return move(array, lambda x, y, c, z: (x ^ 1, y, c, z))


def to_rows(array, first):
    def target(x, y, c, z):
        h, p = x // 2, x % 2
        return 2 * p + (h if first else 1 - h), z // 2, c, 2 * ((y - z // 2) % 4) + (z + h) % 2

    return move(array, target)


def after_kernel(n_after, *refs):
    sources, targets = refs[: len(refs) - n_after], refs[len(refs) - n_after :]
    n = 0
    for target in targets:
        for place in range(target.shape[0]):
            target[place] = sources[n][...]
            n += 1


def after(stacks, *earlier):
    pieces = [piece for stack in stacks for piece in stack]
    shapes = [jax.ShapeDtypeStruct((len(stack), *stack[0].shape), BF) for stack in stacks]
    return pl.pallas_call(
        lambda *refs: after_kernel(
            len(stacks), *refs[: len(pieces)], *refs[len(pieces) + len(earlier) :]
        ),
        in_specs=[VMEM] * (len(pieces) + len(earlier)),
        out_specs=[VMEM] * len(stacks),
        out_shape=shapes,
        compiler_params=pltpu.CompilerParams(vmem_limit_bytes=8 * MIB),
        cost_estimate=pl.CostEstimate(flops=0, bytes_accessed=10**6, transcendentals=0),
        name="after",
    )(*pieces, *earlier)


def angles(rows, cols, modulus):
    turned = (np.arange(rows)[:, None] * np.arange(cols)[None, :]) % modulus
    angle = turned.astype(np.float32) * np.float32(2.0 * math.pi / modulus)
    return np.cos(angle), np.sin(angle)


def tables():
    c_one, s_one = angles(128, 64, 128)
    order = np.array([4 * s + q for q in range(4) for s in range(16)])
    c_one, s_one = c_one[:, order], s_one[:, order]
    t_cos, t_sin = angles(128, 128, 16384)
    c_blk, s_blk = angles(128, 128, 128)
    first = np.concatenate([c_one, s_one], 0)
    last = np.concatenate([c_one.T, -s_one.T], 1) / 16384.0
    fwd = np.block([[c_blk, -s_blk], [s_blk, c_blk]])
    bwd = np.block([[c_blk, s_blk], [-s_blk, c_blk]])
    as_bf = [jnp.asarray(t, dtype=F32).astype(BF) for t in (first, last, fwd, bwd)]
    return (*as_bf, jnp.asarray(t_cos, dtype=F32), jnp.asarray(t_sin, dtype=F32))


def prepare_kernel(gate, key, value, filt, out):
    row = lax.broadcasted_iota(jnp.int32, (128, 128), 0)
    col = lax.broadcasted_iota(jnp.int32, (128, 128), 1)
    eye = (row == col).astype(BF)
    mixed = (key[...].astype(F32) * value[...].astype(F32)).astype(BF)
    for place, block in enumerate((mixed, filt[...], gate[...])):
        turned = lax.dot_general(
            eye, block, (((1,), (1,)), ((), ())), preferred_element_type=F32
        ).astype(BF)
        for j in range(4):
            out[j, 32 * place : 32 * place + 32, :] = turned[32 * j : 32 * j + 32, :]


def prepare(gate, key, value, filt):
    block = pl.BlockSpec((512, 128), lambda i: (0, i))
    return pl.pallas_call(
        prepare_kernel,
        grid=(4,),
        in_specs=[block] * 4,
        out_specs=pl.BlockSpec((4, 96, 512), lambda i: (i, 0, 0)),
        out_shape=jax.ShapeDtypeStruct((16, 96, 512), BF),
        name="prepare",
    )(gate, key, value, filt)


GROUP = 8


def conv_kernel(
    where, skip, data, first, last, fwd, bwd, t_cos, t_sin, keep_same, keep_other, send, grid, done
):
    for arr in range(3):
        for half in range(2):
            lo = 32 * arr + 16 * half
            block = data[:, lo : lo + 16, :].astype(F32)
            block = jnp.swapaxes(block, 0, 1).astype(BF)
            for i in range(16):
                for q in range(4):
                    grid[16 * q : 16 * q + 16, (lo + i) * 128 : (lo + i + 1) * 128] = block[
                        i, :, 128 * q : 128 * q + 128
                    ]
    tc = t_cos[...]
    ts = t_sin[...]

    def group(g, carry):
        lanes = pl.ds(pl.multiple_of(g * (GROUP * 128), GROUP * 128), GROUP * 128)
        f_lanes = pl.ds(pl.multiple_of(4096 + g * (GROUP * 128), GROUP * 128), GROUP * 128)
        g_lanes = pl.ds(pl.multiple_of(8192 + g * (GROUP * 128), GROUP * 128), GROUP * 128)
        spectra = []
        for where_lanes in (lanes, f_lanes):
            s = jnp.dot(first[...], grid[:, where_lanes], preferred_element_type=F32)
            rows = []
            for i in range(GROUP):
                s_re = s[:128, 128 * i : 128 * i + 128]
                s_im = -s[128:, 128 * i : 128 * i + 128]
                t_re = (s_re * tc + s_im * ts).astype(BF)
                t_im = (s_im * tc - s_re * ts).astype(BF)
                rows.append(jnp.concatenate([t_re, t_im], 1))
            spectra.append(
                jnp.dot(jnp.concatenate(rows, 0), fwd[...], preferred_element_type=F32)
            )
        u, f = spectra
        u_re, u_im, f_re, f_im = u[:, :128], u[:, 128:], f[:, :128], f[:, 128:]
        p_re = (u_re * f_re - u_im * f_im).astype(BF)
        p_im = (u_re * f_im + u_im * f_re).astype(BF)
        qq = jnp.dot(
            jnp.concatenate([p_re, p_im], 1), bwd[...], preferred_element_type=F32
        )
        cols = []
        for i in range(GROUP):
            q_re = qq[128 * i : 128 * i + 128, :128]
            q_im = qq[128 * i : 128 * i + 128, 128:]
            r_re = (q_re * tc - q_im * ts).astype(BF)
            r_im = (q_im * tc + q_re * ts).astype(BF)
            cols.append(jnp.concatenate([r_re, r_im], 0))
        conv = jnp.dot(last[...], jnp.concatenate(cols, 1), preferred_element_type=F32)
        signal = grid[:, lanes].astype(F32)
        gates = grid[:, g_lanes].astype(F32)
        for i in range(GROUP):
            part = slice(128 * i, 128 * i + 128)
            mixed_out = conv[:, part] + skip[g * GROUP + i] * signal[:, part]
            gated = gates[:, part] * mixed_out.astype(BF).astype(F32)
            done[g * GROUP + i] = gated
        return carry

    lax.fori_loop(0, 32 // GROUP, group, 0)
    core = where[2]
    x_lo = where[0] % 2

    def quarter(lo, part):
        rows = pl.ds(pl.multiple_of(part * 16, 16), 16)
        return jnp.swapaxes(done[lo : lo + 16, rows, :], 0, 1).astype(BF)

    for lo in (0, 16):
        keep_same[:, lo : lo + 16, :] = quarter(lo, 2 * x_lo + core)
        keep_other[:, lo : lo + 16, :] = quarter(lo, 2 * (1 - x_lo) + core)
        send[0, :, lo : lo + 16, :] = quarter(lo, 2 * x_lo + 1 - core)
        send[1, :, lo : lo + 16, :] = quarter(lo, 2 * (1 - x_lo) + 1 - core)


def convolve(where, skips, data):
    piece = jax.ShapeDtypeStruct((16, 32, 128), BF)
    return pl.pallas_call(
        conv_kernel,
        in_specs=[SMEM, SMEM] + [VMEM] * 7,
        out_specs=[VMEM] * 3,
        out_shape=[piece, piece, jax.ShapeDtypeStruct((2, 16, 32, 128), BF)],
        scratch_shapes=[pltpu.VMEM((64, 96 * 128), BF), pltpu.VMEM((32, 64, 128), F32)],
        compiler_params=pltpu.CompilerParams(vmem_limit_bytes=14 * MIB),
        cost_estimate=pl.CostEstimate(
            flops=4 * 10**9, bytes_accessed=3 * 10**6, transcendentals=0
        ),
        name="convolve",
    )(where, skips, data, *tables())


def columns_kernel(where, own, below, above, far_low, far_high, right):
    y, core = where[1], where[2]
    for j in range(2):
        from_x = where[4 + j]
        for step in (0, -1, 1, 2):
            from_y = (y + step + 4) % 4
            base = 32 * (8 * (from_x // 2) + 2 * from_y)
            for rel in range(2):
                row = pl.ds(pl.multiple_of(base + 32 * ((core + rel) % 2), 32), 32)
                if step == 2:
                    piece = (far_low, far_high)[rel].at[j, 0]
                else:
                    piece = {0: own, -1: below, 1: above}[step].at[j, rel]
                for a in range(16):
                    right[row, 128 * a : 128 * a + 128] = piece[a]


def columns(where, *shards):
    return pl.pallas_call(
        columns_kernel,
        in_specs=[SMEM] + [VMEM] * len(shards),
        out_specs=VMEM,
        out_shape=jax.ShapeDtypeStruct((512, 2048), BF),
        compiler_params=pltpu.CompilerParams(vmem_limit_bytes=12 * MIB),
        cost_estimate=pl.CostEstimate(flops=0, bytes_accessed=4 * 10**6, transcendentals=0),
        name="columns",
    )(where, *shards)


def gram_kernel(steps, n_right, n_earlier, where, *refs):
    rows = 64 * len(steps)
    rights, shard_refs = refs[:n_right], refs[n_right : -3 - n_earlier]
    keep, send, left = refs[-3:]
    x, core, z = where[0], where[2], where[3]
    shards = []
    for ref in shard_refs:
        shards += [(ref, j) for j in range(2)] if ref.shape[0] == 2 else [(ref, 0)]
    for n, (ref, j) in enumerate(shards):
        h = (x + n) % 2
        source = (z + steps[n // 2] + 8) % 8
        slot = (source + h + core) % 2
        for rel in range(2):
            row = rows * slot + 64 * (n // 2) + 32 * ((core + rel) % 2)
            row = pl.multiple_of(row, 32)
            for a in range(16):
                left[pl.ds(row, 32), 128 * a : 128 * a + 128] = ref[j, rel, a]
    for half, right in enumerate(rights):
        times(left, right, keep.at[half], send.at[half])


def times(left, right, keep, send):
    rows = keep.shape[0]
    for sub in range(2):
        lanes = slice(256 * sub, 256 * sub + 256)
        part = lax.dot_general(
            left[...],
            right[lanes, :],
            (((1,), (1,)), ((), ())),
            preferred_element_type=F32,
        )
        keep[:, lanes] = part[:rows]
        send[:, lanes] = part[rows:]


def again_kernel(left, right, keep, send):
    times(left, right, keep.at[0], send.at[0])


def gram_again(left, right):
    tile = jax.ShapeDtypeStruct((1, left.shape[0] // 2, 512), F32)
    return pl.pallas_call(
        again_kernel,
        in_specs=[VMEM] * 2,
        out_specs=[VMEM] * 2,
        out_shape=[tile, tile],
        compiler_params=pltpu.CompilerParams(vmem_limit_bytes=18 * MIB),
        cost_estimate=pl.CostEstimate(
            flops=2 * left.shape[0] * 512 * 2048, bytes_accessed=4 * 10**6, transcendentals=0
        ),
        name="gram_again",
    )(left, right)


def gram_part(steps, where, rights, shards, *earlier):
    rows = 64 * len(steps)
    tile = jax.ShapeDtypeStruct((len(rights), rows, 512), F32)
    return pl.pallas_call(
        functools.partial(gram_kernel, steps, len(rights), len(earlier)),
        in_specs=[SMEM] + [VMEM] * (len(rights) + len(shards) + len(earlier)),
        out_specs=[VMEM] * 3,
        out_shape=[tile, tile, jax.ShapeDtypeStruct((2 * rows, 2048), BF)],
        compiler_params=pltpu.CompilerParams(vmem_limit_bytes=18 * MIB),
        cost_estimate=pl.CostEstimate(
            flops=4 * rows * len(rights) * 512 * 2048,
            bytes_accessed=4 * 10**6,
            transcendentals=0,
        ),
        name="gram_part",
    )(where, *rights, *shards, *earlier)


def finish_kernel(chunks, where, running, *refs):
    out = refs[-1]
    y, core, z = where[1], where[2], where[3]
    for n, steps in enumerate(chunks):
        keep, got, theirs = refs[3 * n : 3 * n + 3]
        for k, step in enumerate(steps):
            source = (z + step + 8) % 8
            h = (source + core) % 2
            from_y = (y + source // 2) % 4
            rows = pl.ds(pl.multiple_of(64 * (4 * h + from_y), 64), 64)
            here = slice(64 * k, 64 * k + 64)
            total = keep[0, here, :] + got[0, here, :] + theirs[here, :]
            out[rows, :] = running[rows, :] + total * (1.0 / 8192.0)


def finish(chunks, where, running, *parts):
    specs = [SMEM, VMEM]
    for steps in chunks:
        half = pl.BlockSpec((1, 64 * len(steps), 512), lambda i: (0, 0, 0))
        specs += [half, half, pl.BlockSpec((64 * len(steps), 512), lambda i: (0, 0))]
    return pl.pallas_call(
        functools.partial(finish_kernel, chunks),
        grid=(1,),
        in_specs=specs,
        out_specs=VMEM,
        out_shape=jax.ShapeDtypeStruct((512, 512), F32),
        compiler_params=pltpu.CompilerParams(vmem_limit_bytes=12 * MIB),
        cost_estimate=pl.CostEstimate(flops=10**6, bytes_accessed=5 * 10**6, transcendentals=0),
        name="finish",
    )(where, running, *parts)


STEPS = (0, -1, 1, -2, 2, -3, 3, 4)
CHUNKS = (STEPS[:7], STEPS[7:])


def local(gate_in, key_in, value_in, filt_in, skip_gain, running_gram):
    seq, grp = lax.axis_index("seq"), lax.axis_index("grp")
    x, y, core, z = coords(seq, grp)
    where = jnp.stack([x, y, core, z, x, x]).astype(jnp.int32)
    across = jnp.stack([x, y, core, z, x, (x + 2) % 4]).astype(jnp.int32)
    beside = jnp.stack([x, y, core, z, (x + 1) % 4, (x + 3) % 4]).astype(jnp.int32)
    skips = lax.dynamic_slice_in_dim(skip_gain, seq * 32, 32, 0)

    outgoing = prepare(gate_in, key_in, value_in, filt_in)
    data = lax.all_to_all(outgoing, "seq", split_axis=0, concat_axis=0, tiled=True)
    same, other, send = convolve(where, skips, data)

    got = other_core(send)
    same = jnp.stack([same, got[0]])
    other = jnp.stack([other, got[1]])
    crossed = (x % 2) != (x // 2)
    row_a = to_rows(jnp.where(crossed, other, same), True)
    row_b = to_rows(jnp.where(crossed, same, other), False)
    below = along_x(other, 1)
    above = along_x(other, 3)
    opposite = along_x(same, 2)

    (rows,) = after([[row_a, row_b]])
    (near,) = after([[above, below]], same)
    ups, downs = [rows], [rows]
    for _ in range(3):
        ups.append(along_z(ups[-1], 1))
        downs.append(along_z(downs[-1], 7))
    far = along_z(ups[3][:1], 1), along_z(downs[3][1:], 7)

    near_up, near_down = along_y(near, 1), along_y(near, 3)
    (own,) = after([[same, opposite]], near_up, near_down)
    near_far = along_y(near_up[:, :1], 1), along_y(near_down[:, 1:], 3)
    own_up, own_down = along_y(own, 1), along_y(own, 3)
    own_far = along_y(own_up[:, :1], 1), along_y(own_down[:, 1:], 3)
    right = columns(beside, near, near_up, near_down, *near_far)
    own_right = columns(across, own, own_up, own_down, *own_far)

    early = [rows, ups[1], downs[1], ups[2], downs[2], ups[3], downs[3]]
    keep, send, left = gram_part(CHUNKS[0], where, [right], early, own_right)
    theirs_a = other_x_lo(keep[0] + other_core(send)[0])
    keep_a, send_a = gram_again(left, own_right)
    got_a = other_core(send_a)

    keep_b, send_b, _ = gram_part(CHUNKS[1], where, [own_right, right], far)
    got_b = other_core(send_b)
    theirs_b = other_x_lo(keep_b[1] + got_b[1])
    return finish(
        CHUNKS, where, running_gram, keep_a, got_a, theirs_a, keep_b, got_b, theirs_b
    )


def solution(mesh):
    in_specs = (
        P("seq", "grp"),
        P("seq", "grp"),
        P("seq", "grp"),
        P("seq", "grp"),
        P("grp"),
        P("seq", "grp"),
    )
    out_specs = P("seq", "grp")
    return jax.shard_map(local, mesh=mesh, in_specs=in_specs, out_specs=out_specs, check_vma=False)
```

```python
import functools
import math

import jax
import jax.numpy as jnp
import numpy as np
from jax import lax
from jax.experimental import pallas as pl
from jax.experimental.pallas import tpu as pltpu
from jax.sharding import PartitionSpec as P

BF = jnp.bfloat16
F32 = jnp.float32
MESH = ("seq", "grp")
VMEM = pl.BlockSpec(memory_space=pltpu.VMEM)
SMEM = pl.BlockSpec(memory_space=pltpu.SMEM)
MIB = 1024 * 1024


def coords(seq, grp):
    return 2 * (seq // 8) + grp // 8, (seq // 2) % 4, seq % 2, grp % 8


def device(x, y, core, z):
    return (8 * (x // 2) + 2 * y + core) * 16 + 8 * (x % 2) + z


def move(array, target):
    pairs = []
    for seq in range(16):
        for grp in range(16):
            pairs.append((16 * seq + grp, device(*target(*coords(seq, grp)))))
    return lax.ppermute(array, MESH, pairs)


def along_x(array, step):
    return move(array, lambda x, y, c, z: ((x + step) % 4, y, c, z))


def along_y(array, step):
    return move(array, lambda x, y, c, z: (x, (y + step) % 4, c, z))


def along_z(array, step):
    return move(array, lambda x, y, c, z: (x, y, c, (z + step) % 8))


def other_core(array):
    return move(array, lambda x, y, c, z: (x, y, 1 - c, z))


def other_x_lo(array):
    return move(array, lambda x, y, c, z: (x ^ 1, y, c, z))


def to_rows(array, first):
    def target(x, y, c, z):
        h, p = x // 2, x % 2
        return 2 * p + (h if first else 1 - h), z // 2, c, 2 * ((y - z // 2) % 4) + (z + h) % 2

    return move(array, target)


def after_kernel(n_after, *refs):
    sources, targets = refs[: len(refs) - n_after], refs[len(refs) - n_after :]
    n = 0
    for target in targets:
        for place in range(target.shape[0]):
            target[place] = sources[n][...]
            n += 1


def after(stacks, *earlier):
    pieces = [piece for stack in stacks for piece in stack]
    shapes = [jax.ShapeDtypeStruct((len(stack), *stack[0].shape), BF) for stack in stacks]
    return pl.pallas_call(
        lambda *refs: after_kernel(
            len(stacks), *refs[: len(pieces)], *refs[len(pieces) + len(earlier) :]
        ),
        in_specs=[VMEM] * (len(pieces) + len(earlier)),
        out_specs=[VMEM] * len(stacks),
        out_shape=shapes,
        compiler_params=pltpu.CompilerParams(vmem_limit_bytes=8 * MIB),
        cost_estimate=pl.CostEstimate(flops=0, bytes_accessed=10**6, transcendentals=0),
        name="after",
    )(*pieces, *earlier)


def angles(rows, cols, modulus):
    turned = (np.arange(rows)[:, None] * np.arange(cols)[None, :]) % modulus
    angle = turned.astype(np.float32) * np.float32(2.0 * math.pi / modulus)
    return np.cos(angle), np.sin(angle)


def tables():
    c_one, s_one = angles(128, 64, 128)
    order = np.array([4 * s + q for q in range(4) for s in range(16)])
    c_one, s_one = c_one[:, order], s_one[:, order]
    t_cos, t_sin = angles(128, 128, 16384)
    c_blk, s_blk = angles(128, 128, 128)
    first = np.concatenate([c_one, s_one], 0)
    last = np.concatenate([c_one.T, -s_one.T], 1) / 16384.0
    fwd = np.block([[c_blk, -s_blk], [s_blk, c_blk]])
    bwd = np.block([[c_blk, s_blk], [-s_blk, c_blk]])
    as_bf = [jnp.asarray(t, dtype=F32).astype(BF) for t in (first, last, fwd, bwd)]
    return (*as_bf, jnp.asarray(t_cos, dtype=F32), jnp.asarray(t_sin, dtype=F32))


def prepare_kernel(gate, key, value, filt, out):
    row = lax.broadcasted_iota(jnp.int32, (128, 128), 0)
    col = lax.broadcasted_iota(jnp.int32, (128, 128), 1)
    eye = (row == col).astype(BF)
    mixed = (key[...].astype(F32) * value[...].astype(F32)).astype(BF)
    for place, block in enumerate((mixed, filt[...], gate[...])):
        turned = lax.dot_general(
            eye, block, (((1,), (1,)), ((), ())), preferred_element_type=F32
        ).astype(BF)
        for j in range(4):
            out[j, 32 * place : 32 * place + 32, :] = turned[32 * j : 32 * j + 32, :]


def prepare(gate, key, value, filt):
    block = pl.BlockSpec((512, 128), lambda i: (0, i))
    return pl.pallas_call(
        prepare_kernel,
        grid=(4,),
        in_specs=[block] * 4,
        out_specs=pl.BlockSpec((4, 96, 512), lambda i: (i, 0, 0)),
        out_shape=jax.ShapeDtypeStruct((16, 96, 512), BF),
        name="prepare",
    )(gate, key, value, filt)


GROUP = 8


def conv_kernel(
    where, skip, data, first, last, fwd, bwd, t_cos, t_sin, keep_same, keep_other, send, grid, done
):
    for arr in range(3):
        for half in range(2):
            lo = 32 * arr + 16 * half
            block = data[:, lo : lo + 16, :].astype(F32)
            block = jnp.swapaxes(block, 0, 1).astype(BF)
            for i in range(16):
                for q in range(4):
                    grid[16 * q : 16 * q + 16, (lo + i) * 128 : (lo + i + 1) * 128] = block[
                        i, :, 128 * q : 128 * q + 128
                    ]
    tc = t_cos[...]
    ts = t_sin[...]

    def group(g, carry):
        lanes = pl.ds(pl.multiple_of(g * (GROUP * 128), GROUP * 128), GROUP * 128)
        f_lanes = pl.ds(pl.multiple_of(4096 + g * (GROUP * 128), GROUP * 128), GROUP * 128)
        g_lanes = pl.ds(pl.multiple_of(8192 + g * (GROUP * 128), GROUP * 128), GROUP * 128)
        spectra = []
        for where_lanes in (lanes, f_lanes):
            s = jnp.dot(first[...], grid[:, where_lanes], preferred_element_type=F32)
            rows = []
            for i in range(GROUP):
                s_re = s[:128, 128 * i : 128 * i + 128]
                s_im = -s[128:, 128 * i : 128 * i + 128]
                t_re = (s_re * tc + s_im * ts).astype(BF)
                t_im = (s_im * tc - s_re * ts).astype(BF)
                rows.append(jnp.concatenate([t_re, t_im], 1))
            spectra.append(
                jnp.dot(jnp.concatenate(rows, 0), fwd[...], preferred_element_type=F32)
            )
        u, f = spectra
        u_re, u_im, f_re, f_im = u[:, :128], u[:, 128:], f[:, :128], f[:, 128:]
        p_re = (u_re * f_re - u_im * f_im).astype(BF)
        p_im = (u_re * f_im + u_im * f_re).astype(BF)
        qq = jnp.dot(
            jnp.concatenate([p_re, p_im], 1), bwd[...], preferred_element_type=F32
        )
        cols = []
        for i in range(GROUP):
            q_re = qq[128 * i : 128 * i + 128, :128]
            q_im = qq[128 * i : 128 * i + 128, 128:]
            r_re = (q_re * tc - q_im * ts).astype(BF)
            r_im = (q_im * tc + q_re * ts).astype(BF)
            cols.append(jnp.concatenate([r_re, r_im], 0))
        conv = jnp.dot(last[...], jnp.concatenate(cols, 1), preferred_element_type=F32)
        signal = grid[:, lanes].astype(F32)
        gates = grid[:, g_lanes].astype(F32)
        for i in range(GROUP):
            part = slice(128 * i, 128 * i + 128)
            mixed_out = conv[:, part] + skip[g * GROUP + i] * signal[:, part]
            gated = gates[:, part] * mixed_out.astype(BF).astype(F32)
            done[g * GROUP + i] = gated
        return carry

    lax.fori_loop(0, 32 // GROUP, group, 0)
    core = where[2]
    x_lo = where[0] % 2

    def quarter(lo, part):
        rows = pl.ds(pl.multiple_of(part * 16, 16), 16)
        return jnp.swapaxes(done[lo : lo + 16, rows, :], 0, 1).astype(BF)

    for lo in (0, 16):
        keep_same[:, lo : lo + 16, :] = quarter(lo, 2 * x_lo + core)
        keep_other[:, lo : lo + 16, :] = quarter(lo, 2 * (1 - x_lo) + core)
        send[0, :, lo : lo + 16, :] = quarter(lo, 2 * x_lo + 1 - core)
        send[1, :, lo : lo + 16, :] = quarter(lo, 2 * (1 - x_lo) + 1 - core)


def convolve(where, skips, data):
    piece = jax.ShapeDtypeStruct((16, 32, 128), BF)
    return pl.pallas_call(
        conv_kernel,
        in_specs=[SMEM, SMEM] + [VMEM] * 7,
        out_specs=[VMEM] * 3,
        out_shape=[piece, piece, jax.ShapeDtypeStruct((2, 16, 32, 128), BF)],
        scratch_shapes=[pltpu.VMEM((64, 96 * 128), BF), pltpu.VMEM((32, 64, 128), F32)],
        compiler_params=pltpu.CompilerParams(vmem_limit_bytes=14 * MIB),
        cost_estimate=pl.CostEstimate(
            flops=4 * 10**9, bytes_accessed=3 * 10**6, transcendentals=0
        ),
        name="convolve",
    )(where, skips, data, *tables())


def columns_kernel(where, own, below, above, far_low, far_high, right):
    y, core = where[1], where[2]
    for j in range(2):
        from_x = where[4 + j]
        for step in (0, -1, 1, 2):
            from_y = (y + step + 4) % 4
            base = 32 * (8 * (from_x // 2) + 2 * from_y)
            for rel in range(2):
                row = pl.ds(pl.multiple_of(base + 32 * ((core + rel) % 2), 32), 32)
                if step == 2:
                    piece = (far_low, far_high)[rel].at[j, 0]
                else:
                    piece = {0: own, -1: below, 1: above}[step].at[j, rel]
                for a in range(16):
                    right[row, 128 * a : 128 * a + 128] = piece[a]


def columns(where, *shards):
    return pl.pallas_call(
        columns_kernel,
        in_specs=[SMEM] + [VMEM] * len(shards),
        out_specs=VMEM,
        out_shape=jax.ShapeDtypeStruct((512, 2048), BF),
        compiler_params=pltpu.CompilerParams(vmem_limit_bytes=12 * MIB),
        cost_estimate=pl.CostEstimate(flops=0, bytes_accessed=4 * 10**6, transcendentals=0),
        name="columns",
    )(where, *shards)


def gram_kernel(steps, n_right, n_earlier, where, *refs):
    rows = 64 * len(steps)
    rights, shard_refs = refs[:n_right], refs[n_right : -3 - n_earlier]
    keep, send, left = refs[-3:]
    x, core, z = where[0], where[2], where[3]
    shards = []
    for ref in shard_refs:
        shards += [(ref, j) for j in range(2)] if ref.shape[0] == 2 else [(ref, 0)]
    for n, (ref, j) in enumerate(shards):
        h = (x + n) % 2
        source = (z + steps[n // 2] + 8) % 8
        slot = (source + h + core) % 2
        for rel in range(2):
            row = rows * slot + 64 * (n // 2) + 32 * ((core + rel) % 2)
            row = pl.multiple_of(row, 32)
            for a in range(16):
                left[pl.ds(row, 32), 128 * a : 128 * a + 128] = ref[j, rel, a]
    for half, right in enumerate(rights):
        times(left, right, keep.at[half], send.at[half])


def times(left, right, keep, send):
    rows = keep.shape[0]
    for sub in range(2):
        lanes = slice(256 * sub, 256 * sub + 256)
        part = lax.dot_general(
            left[...],
            right[lanes, :],
            (((1,), (1,)), ((), ())),
            preferred_element_type=F32,
        )
        keep[:, lanes] = part[:rows]
        send[:, lanes] = part[rows:]


def again_kernel(left, right, keep, send):
    times(left, right, keep.at[0], send.at[0])


def gram_again(left, right):
    tile = jax.ShapeDtypeStruct((1, left.shape[0] // 2, 512), F32)
    return pl.pallas_call(
        again_kernel,
        in_specs=[VMEM] * 2,
        out_specs=[VMEM] * 2,
        out_shape=[tile, tile],
        compiler_params=pltpu.CompilerParams(vmem_limit_bytes=18 * MIB),
        cost_estimate=pl.CostEstimate(flops=10**6, bytes_accessed=10**4, transcendentals=0),
        name="gram_again",
    )(left, right)


def gram_part(steps, where, rights, shards, *earlier):
    rows = 64 * len(steps)
    tile = jax.ShapeDtypeStruct((len(rights), rows, 512), F32)
    return pl.pallas_call(
        functools.partial(gram_kernel, steps, len(rights), len(earlier)),
        in_specs=[SMEM] + [VMEM] * (len(rights) + len(shards) + len(earlier)),
        out_specs=[VMEM] * 3,
        out_shape=[tile, tile, jax.ShapeDtypeStruct((2 * rows, 2048), BF)],
        compiler_params=pltpu.CompilerParams(vmem_limit_bytes=18 * MIB),
        cost_estimate=pl.CostEstimate(flops=10**6, bytes_accessed=10**4, transcendentals=0),
        name="gram_part",
    )(where, *rights, *shards, *earlier)


def finish_kernel(chunks, where, running, *refs):
    out = refs[-1]
    y, core, z = where[1], where[2], where[3]
    for n, steps in enumerate(chunks):
        keep, got, theirs = refs[3 * n : 3 * n + 3]
        for k, step in enumerate(steps):
            source = (z + step + 8) % 8
            h = (source + core) % 2
            from_y = (y + source // 2) % 4
            rows = pl.ds(pl.multiple_of(64 * (4 * h + from_y), 64), 64)
            here = slice(64 * k, 64 * k + 64)
            total = keep[0, here, :] + got[0, here, :] + theirs[here, :]
            out[rows, :] = running[rows, :] + total * (1.0 / 8192.0)


def finish(chunks, where, running, *parts):
    specs = [SMEM, VMEM]
    for steps in chunks:
        half = pl.BlockSpec((1, 64 * len(steps), 512), lambda i: (0, 0, 0))
        specs += [half, half, pl.BlockSpec((64 * len(steps), 512), lambda i: (0, 0))]
    return pl.pallas_call(
        functools.partial(finish_kernel, chunks),
        grid=(1,),
        in_specs=specs,
        out_specs=VMEM,
        out_shape=jax.ShapeDtypeStruct((512, 512), F32),
        compiler_params=pltpu.CompilerParams(vmem_limit_bytes=12 * MIB),
        cost_estimate=pl.CostEstimate(flops=10**6, bytes_accessed=5 * 10**6, transcendentals=0),
        name="finish",
    )(where, running, *parts)


STEPS = (0, -1, 1, -2, 2, -3, 3, 4)
CHUNKS = (STEPS[:7], STEPS[7:])


def local(gate_in, key_in, value_in, filt_in, skip_gain, running_gram):
    seq, grp = lax.axis_index("seq"), lax.axis_index("grp")
    x, y, core, z = coords(seq, grp)
    where = jnp.stack([x, y, core, z, x, x]).astype(jnp.int32)
    across = jnp.stack([x, y, core, z, x, (x + 2) % 4]).astype(jnp.int32)
    beside = jnp.stack([x, y, core, z, (x + 1) % 4, (x + 3) % 4]).astype(jnp.int32)
    skips = lax.dynamic_slice_in_dim(skip_gain, seq * 32, 32, 0)

    outgoing = prepare(gate_in, key_in, value_in, filt_in)
    data = lax.all_to_all(outgoing, "seq", split_axis=0, concat_axis=0, tiled=True)
    same, other, send = convolve(where, skips, data)

    got = other_core(send)
    same = jnp.stack([same, got[0]])
    other = jnp.stack([other, got[1]])
    crossed = (x % 2) != (x // 2)
    row_a = to_rows(jnp.where(crossed, other, same), True)
    row_b = to_rows(jnp.where(crossed, same, other), False)
    below = along_x(other, 1)
    above = along_x(other, 3)
    opposite = along_x(same, 2)

    (rows,) = after([[row_a, row_b]])
    (near,) = after([[above, below]], same)
    ups, downs = [rows], [rows]
    for _ in range(3):
        ups.append(along_z(ups[-1], 1))
        downs.append(along_z(downs[-1], 7))
    far = along_z(ups[3][:1], 1), along_z(downs[3][1:], 7)

    near_up, near_down = along_y(near, 1), along_y(near, 3)
    (own,) = after([[same, opposite]], near_up, near_down)
    near_far = along_y(near_up[:, :1], 1), along_y(near_down[:, 1:], 3)
    own_up, own_down = along_y(own, 1), along_y(own, 3)
    own_far = along_y(own_up[:, :1], 1), along_y(own_down[:, 1:], 3)
    right = columns(beside, near, near_up, near_down, *near_far)
    own_right = columns(across, own, own_up, own_down, *own_far)

    early = [rows, ups[1], downs[1], ups[2], downs[2], ups[3], downs[3]]
    keep, send, left = gram_part(CHUNKS[0], where, [right], early, own_right)
    theirs_a = other_x_lo(keep[0] + other_core(send)[0])
    keep_a, send_a = gram_again(left, own_right)
    got_a = other_core(send_a)

    keep_b, send_b, _ = gram_part(CHUNKS[1], where, [own_right, right], far)
    got_b = other_core(send_b)
    theirs_b = other_x_lo(keep_b[1] + got_b[1])
    return finish(
        CHUNKS, where, running_gram, keep_a, got_a, theirs_a, keep_b, got_b, theirs_b
    )


def solution(mesh):
    in_specs = (
        P("seq", "grp"),
        P("seq", "grp"),
        P("seq", "grp"),
        P("seq", "grp"),
        P("grp"),
        P("seq", "grp"),
    )
    out_specs = P("seq", "grp")
    return jax.shard_map(local, mesh=mesh, in_specs=in_specs, out_specs=out_specs, check_vma=False)
```
